128 devices in a mesh: section: 2 (over y_lo), gx: 8 (over x, y_hi), gy: 8 (over z, core).
Axes of the slice: x: 4, y: 4 (y_hi: 2, y_lo: 2; y = y_hi * 2 + y_lo), z: 4, core: 2. Of those that a mesh axis runs over, the one named last changes fastest.
Arguments:
- images: bfloat16 [2, 2, 640, 1024], P(None, None, 'gx', 'gy'), may hold values from -6 to 6
- counts: int32 [2], replicated, may hold values from 1 to 2, as said below
- attn_gain: float32 [2, 1024], P('section', 'gy'), may hold values from 0.5 to 1.5
- attn_shift: float32 [2, 1024], P('section', 'gy'), may hold values from -1.75 to 1.75
- w_query: bfloat16 [2, 1024, 1024], P('section', 'gx', 'gy'), may hold values from -0.1875 to 0.1875
- b_query: float32 [2, 1024], P('section', 'gy'), may hold values from -1.75 to 1.75
- w_key: bfloat16 [2, 1024, 1024], P('section', 'gx', 'gy'), may hold values from -0.1875 to 0.1875
- w_value: bfloat16 [2, 1024, 1024], P('section', 'gx', 'gy'), may hold values from -0.1875 to 0.1875
- b_value: float32 [2, 1024], P('section', 'gy'), may hold values from -1.75 to 1.75
- w_out: bfloat16 [2, 1024, 1024], P('section', 'gy', 'gx'), may hold values from -1 to 1
- b_out: float32 [2, 1024], P('section', 'gy'), may hold values from -1.75 to 1.75
- mlp_gain: float32 [2, 1024], P('section', 'gy'), may hold values from 0.5 to 1.5
- mlp_shift: float32 [2, 1024], P('section', 'gy'), may hold values from -1.75 to 1.75
- w_up: bfloat16 [2, 1024, 4096], P('section', 'gx', 'gy'), may hold values from -0.1875 to 0.1875
- b_up: float32 [2, 4096], P('section', 'gy'), may hold values from -1.75 to 1.75
- w_down: bfloat16 [2, 4096, 1024], P('section', 'gy', 'gx'), may hold values from -0.09375 to 0.09375
- b_down: float32 [2, 1024], P('section', 'gy'), may hold values from -1.75 to 1.75
- cotangent: bfloat16 [2, 2, 640, 1024], P(None, None, 'gx', 'gy'), may hold values from -6 to 6
Outputs:
- activations: bfloat16 [2, 2, 2, 640, 1024], P('section', None, None, 'gx', 'gy')
- input_grads: float32 [2, 2, 2, 640, 1024], P('section', None, None, 'gx', 'gy')
- grad_attn_gain: float32 [2, 1024], P('section', 'gy')
- grad_attn_shift: float32 [2, 1024], P('section', 'gy')
- grad_w_query: float32 [2, 1024, 1024], P('section', 'gx', 'gy')
- grad_b_query: float32 [2, 1024], P('section', 'gy')
- grad_w_key: float32 [2, 1024, 1024], P('section', 'gx', 'gy')
- grad_w_value: float32 [2, 1024, 1024], P('section', 'gx', 'gy')
- grad_b_value: float32 [2, 1024], P('section', 'gy')
- grad_w_out: float32 [2, 1024, 1024], P('section', 'gy', 'gx')
- grad_b_out: float32 [2, 1024], P('section', 'gy')
- grad_mlp_gain: float32 [2, 1024], P('section', 'gy')
- grad_mlp_shift: float32 [2, 1024], P('section', 'gy')
- grad_w_up: float32 [2, 1024, 4096], P('section', 'gx', 'gy')
- grad_b_up: float32 [2, 4096], P('section', 'gy')
- grad_w_down: float32 [2, 4096, 1024], P('section', 'gy', 'gx')
- grad_b_down: float32 [2, 1024], P('section', 'gy')
The draws below stay inside these ranges and needn't reach their ends.
Inputs may be any that keep to these rules, and one draw needn't show every extreme that they name: `counts`: each micro-batch holds 1 to 2 images in its first slots; some micro-batch holds 2.
All inputs are finite; a program needn't handle non-finite values.
Results may differ from the reference program's by a relative error of at most 0.02.
Values may be sent and summed in bfloat16 or wider, within the bound.
A program may use at most 128 MiB of HBM per device.

```python
import jax
import jax.numpy as jnp
from jax import lax

D = 1024
HEADS = 16
DH = 64
FF = 4096
SEQ = 577
CAP = 2
MICRO = 2
SEQP = 640


def draw_counts(key, part):
    key = jax.random.fold_in(key, 7)
    key_base, key_full = jax.random.split(key, 2)
    chosen = jax.random.randint(key_base, (MICRO,), 1, CAP + 1)
    full_slot = jax.random.randint(key_full, (), 0, MICRO)
    slots = jnp.arange(MICRO)
    return jnp.where(slots == full_slot, CAP, chosen).astype(jnp.int32)


def steps_of(rng, dims, shards, low, high):
    def one(position, parts):
        draws = jax.random.uniform(jax.random.fold_in(jax.random.fold_in(rng, 6), position), (parts,), jnp.float32, low / len(shards), high / len(shards))
        return jnp.repeat(jnp.exp(draws), dims[position] // parts).reshape((-1,) + (1,) * (len(dims) - position - 1))

    level = one(*shards[0])
    for cut in shards[1:]:
        level = level * one(*cut)
    return level


def gaussian(rng, dims, deviation, limit, shards=(), dtype=jnp.bfloat16):
    array = deviation * jax.random.normal(rng, dims, jnp.float32)
    if shards:
        array = array * steps_of(rng, dims, shards, -0.22, 0.18)
    return jnp.clip(array, -limit, limit).astype(dtype)


def setup_inputs(seed: int = 0) -> dict:
    key_of = jax.random.split(jax.random.key(seed), 19)
    images = gaussian(key_of[0], (MICRO, CAP, SEQP, D), 1.0, 6.0, ((2, 8), (3, 8)))
    counts = draw_counts(jax.random.fold_in(key_of[18], 71), 0)
    attn_gain = jnp.clip(1.0 + 0.1 * jax.random.normal(key_of[2], (2, D), jnp.float32), 0.5, 1.5)
    attn_shift = gaussian(key_of[3], (2, D), 0.3, 1.75, ((0, 2), (1, 8)), jnp.float32)
    w_query = gaussian(key_of[4], (2, D, D), D ** -0.5, 0.1875, ((0, 2), (1, 8), (2, 8)))
    b_query = gaussian(key_of[5], (2, D), 0.3, 1.75, ((0, 2), (1, 8)), jnp.float32)
    w_key = gaussian(key_of[6], (2, D, D), D ** -0.5, 0.1875, ((0, 2), (1, 8), (2, 8)))
    w_value = gaussian(key_of[7], (2, D, D), D ** -0.5, 0.1875, ((0, 2), (1, 8), (2, 8)))
    b_value = gaussian(key_of[8], (2, D), 0.3, 1.75, ((0, 2), (1, 8)), jnp.float32)
    w_out = gaussian(key_of[9], (2, D, D), (D // 32) ** -0.5, 1.0, ((0, 2), (1, 8), (2, 8)))
    b_out = gaussian(key_of[10], (2, D), 0.3, 1.75, ((0, 2), (1, 8)), jnp.float32)
    mlp_gain = jnp.clip(1.0 + 0.1 * jax.random.normal(key_of[11], (2, D), jnp.float32), 0.5, 1.5)
    mlp_shift = gaussian(key_of[12], (2, D), 0.3, 1.75, ((0, 2), (1, 8)), jnp.float32)
    w_up = gaussian(key_of[13], (2, D, FF), D ** -0.5, 0.1875, ((0, 2), (1, 8), (2, 8)))
    b_up = gaussian(key_of[14], (2, FF), 0.3, 1.75, ((0, 2), (1, 8)), jnp.float32)
    w_down = gaussian(key_of[15], (2, FF, D), FF ** -0.5, 0.09375, ((0, 2), (1, 8), (2, 8)))
    b_down = gaussian(key_of[16], (2, D), 0.3, 1.75, ((0, 2), (1, 8)), jnp.float32)
    cotangent = gaussian(key_of[17], (MICRO, CAP, SEQP, D), 1.0, 6.0, ((2, 8), (3, 8)))
    return {"images": images, "counts": counts, "attn_gain": attn_gain, "attn_shift": attn_shift, "w_query": w_query, "b_query": b_query, "w_key": w_key, "w_value": w_value, "b_value": b_value, "w_out": w_out, "b_out": b_out, "mlp_gain": mlp_gain, "mlp_shift": mlp_shift, "w_up": w_up, "b_up": b_up, "w_down": w_down, "b_down": b_down, "cotangent": cotangent}


EPSILON = 1e-06

@jax.custom_vjp
def low(v):
    return lax.optimization_barrier(v.astype(jnp.bfloat16)).astype(jnp.float32)

@jax.custom_vjp
def low_back(v):
    return v

def low_keep(v):
    return (low(v), None)

def low_pass(kept, grad):
    return (grad,)

def back_keep(v):
    return (v, None)

def back_low(kept, grad):
    return (low(grad),)
low.defvjp(low_keep, low_pass)
low_back.defvjp(back_keep, back_low)

def matmul_high(left_side, right_side):
    return jnp.matmul(left_side, right_side, precision=lax.Precision.HIGHEST)

def layer_norm(values, gain_row, shift_row):
    center = values - lax.optimization_barrier(jnp.mean(values, axis=-1, keepdims=True))
    spread = lax.optimization_barrier(jnp.mean(center * center, axis=-1, keepdims=True))
    return center * lax.rsqrt(spread + EPSILON) * gain_row + shift_row

def attend_image(image_block):
    queries, keys_in, values_in = image_block
    scores = low_back(jnp.einsum('qhd,khd->hqk', queries, keys_in, precision=lax.Precision.HIGHEST) * DH ** (-0.5))
    key_valid = jnp.arange(SEQP) < SEQ
    masked = jnp.where(key_valid[None, None, :], scores, -1e+30)
    highest = lax.optimization_barrier(jnp.max(masked, axis=-1, keepdims=True))
    exponent = jnp.exp(masked - highest)
    weights = low(exponent / lax.optimization_barrier(jnp.sum(exponent, axis=-1, keepdims=True)))
    return jnp.einsum('hqk,khd->qhd', weights, values_in, precision=lax.Precision.HIGHEST)

def layer_forward(params, inputs):
    attn_gain, attn_shift, w_query, b_query, w_key, w_value, b_value, w_out, b_out, mlp_gain, mlp_shift, w_up, b_up, w_down, b_down = params
    normed = low(layer_norm(inputs, attn_gain, attn_shift))
    queries = low_back(low(matmul_high(normed, w_query) + b_query))
    keys_all = low_back(low(matmul_high(normed, w_key)))
    values_all = low_back(low(matmul_high(normed, w_value) + b_value))
    shape_four = (CAP, SEQP, HEADS, DH)
    mixed_heads = lax.map(jax.checkpoint(attend_image), (queries.reshape(shape_four), keys_all.reshape(shape_four), values_all.reshape(shape_four)))
    mixed_heads = low_back(low(mixed_heads.reshape(CAP, SEQP, D)))
    branch_one = low_back(matmul_high(mixed_heads, w_out))
    middle = inputs + branch_one + b_out
    normed_two = low(layer_norm(middle, mlp_gain, mlp_shift))
    hidden_pre = low_back(matmul_high(normed_two, w_up) + b_up)
    hidden = low(jax.nn.gelu(hidden_pre, approximate=False))
    branch_two = low_back(matmul_high(hidden, w_down))
    return middle + branch_two + b_down

def reference(images, counts, attn_gain, attn_shift, w_query, b_query, w_key, w_value, b_value, w_out, b_out, mlp_gain, mlp_shift, w_up, b_up, w_down, b_down, cotangent):
    stacked = (attn_gain, attn_shift, w_query, b_query, w_key, w_value, b_value, w_out, b_out, mlp_gain, mlp_shift, w_up, b_up, w_down, b_down)
    first_params = tuple((item[0].astype(jnp.float32) for item in stacked))
    second_params = tuple((item[1].astype(jnp.float32) for item in stacked))
    first_sums = tuple((jnp.zeros(item.shape, jnp.float32) for item in first_params))
    second_sums = tuple((jnp.zeros(item.shape, jnp.float32) for item in second_params))
    position_ok = jnp.arange(SEQP) < SEQ
    outs_first = []
    outs_second = []
    grads_first = []
    grads_second = []
    for micro_no in range(MICRO):
        inputs = images[micro_no].astype(jnp.float32)
        out_first, back_first = jax.vjp(layer_forward, first_params, inputs)
        passed = low(out_first)
        out_second, back_second = jax.vjp(layer_forward, second_params, passed)
        rows_ok = (jnp.arange(CAP)[:, None] < counts[micro_no]) & position_ok[None, :]
        seed_grad = cotangent[micro_no].astype(jnp.float32) * rows_ok[:, :, None].astype(jnp.float32)
        param_second, into_second = back_second(seed_grad)
        param_first, into_first = back_first(low(into_second))
        first_sums = jax.tree.map(lambda acc, new: acc + new, first_sums, param_first)
        second_sums = jax.tree.map(lambda acc, new: acc + new, second_sums, param_second)
        outs_first.append(out_first)
        outs_second.append(out_second)
        grads_first.append(into_first)
        grads_second.append(into_second)
    activations = jnp.stack([jnp.stack(outs_first), jnp.stack(outs_second)]).astype(jnp.bfloat16)
    input_grads = jnp.stack([jnp.stack(grads_first), jnp.stack(grads_second)])
    paired = [jnp.stack([one_grad, two_grad]) for one_grad, two_grad in zip(first_sums, second_sums)]
    return (activations, input_grads, paired[0], paired[1], paired[2], paired[3], paired[4], paired[5], paired[6], paired[7], paired[8], paired[9], paired[10], paired[11], paired[12], paired[13], paired[14])
```

```python
import jax
import jax.numpy as jnp
from jax import lax
from jax.experimental import pallas as pl
from jax.experimental.pallas import tpu as pltpu
from jax.sharding import PartitionSpec as P

BF = jnp.bfloat16
F32 = jnp.float32
SEQ = 577
EPS = 1e-06
NEG = -1e30
ROWS = 160
TOK = 80
LANES = 128
WIDE = 1024
MESH = pl.DeviceIdType.MESH

K_X, K_O, K_M, K_D, K_G, K_N2, K_GM, K_N1 = range(8)
V_AG, V_AS, V_MG, V_MS, V_BQ, V_BV, V_BO, V_BD, V_BU = range(9)


def dot_nn(a, b):
    return lax.dot_general(a, b, (((1,), (0,)), ((), ())), preferred_element_type=F32)


def dot_nt(a, b):
    return lax.dot_general(a, b, (((1,), (1,)), ((), ())), preferred_element_type=F32)


def dot_tn(a, b):
    return lax.dot_general(a, b, (((0,), (0,)), ((), ())), preferred_element_type=F32)


def lanes(index):
    return pl.ds(pl.multiple_of(index * LANES, LANES), LANES)


def wait_bytes(ref, sem):
    pltpu.make_async_copy(ref, ref, sem).wait()


def put(src, dst, send_sem, recv_sem, device):
    pltpu.make_async_remote_copy(
        src_ref=src,
        dst_ref=dst,
        send_sem=send_sem,
        recv_sem=recv_sem,
        device_id=device,
        device_id_type=MESH,
    ).start()


def row_sum(values):
    return jnp.sum(values, axis=0, keepdims=True)


def three_parts(values):
    high = values.astype(BF).astype(F32)
    rest = values - high
    mid = rest.astype(BF).astype(F32)
    return high, mid, rest - mid


def kernel(
    images, counts, attn_gain, attn_shift, w_query, b_query, w_key, w_value, b_value, w_out,
    b_out, mlp_gain, mlp_shift, w_up, b_up, w_down, b_down, cotangent,
    act_o, ig_o, g_attn_gain, g_attn_shift, g_w_query, g_b_query, g_w_key, g_w_value, g_b_value,
    g_w_out, g_b_out, g_mlp_gain, g_mlp_shift, g_w_up, g_b_up, g_w_down, g_b_down,
    vec, cot, wqkv, wo, wup, wdn,
    xg, mg, gg, gmg, norm, unit, rstd, res, mid, gcur, gmid,
    stage, rsb, stat, kv, qg, dog, owna, attn_f, attn_b, aux, hid, pre,
    rest, ybuf, igbuf, s_dn, s_up, s_wo, s_qkv, s_vec, r_dn, r_up, r_wo, r_qkv, r_vec, vgrad,
    lsem, gy_send, gy_recv, st_send, st_recv, kv_send, kv_recv, do_send, do_recv,
    vec_send, vec_recv, w_send, w_recv, g_send, g_recv, a_send, a_recv, i_send, i_recv,
):
    s = lax.axis_index("section")
    gx = lax.axis_index("gx")
    gy = lax.axis_index("gy")
    other = 1 - s
    mine = lanes(gy)
    gx_lanes = lanes(gx)
    gx_rows = lanes(gx)

    barrier = pltpu.get_barrier_semaphore()

    def greet(device):
        pl.semaphore_signal(barrier, inc=1, device_id=device, device_id_type=MESH)

    gy_peers = [(s, gx, lax.rem(gy + k, 8)) for k in range(1, 8)]
    gx_peers = [(s, lax.rem(gx + k, 8), gy) for k in range(1, 8)]
    far_gx = [(other, lax.rem(gx + k, 8), gy) for k in range(8)]
    far_gy = [(other, gx, lax.rem(gy + k, 8)) for k in range(8)]
    for device in gy_peers + gx_peers + far_gx + far_gy[1:]:
        greet(device)

    own = [pltpu.make_async_copy(images.at[s], xg.at[0, :, mine], lsem.at[0])]
    own.append(pltpu.make_async_copy(cotangent.at[s], cot, lsem.at[1]))
    rows = [attn_gain, attn_shift, mlp_gain, mlp_shift, b_query, b_value, b_out, b_down]
    vec_own = []
    for row, ref in enumerate(rows):
        vec_own.append(pltpu.make_async_copy(ref, vec.at[s, row, :, mine], lsem.at[8 + row]))
    for part in range(4):
        vec_own.append(
            pltpu.make_async_copy(
                b_up.at[:, part * LANES : (part + 1) * LANES],
                vec.at[s, V_BU + part, :, mine],
                lsem.at[16 + part],
            )
        )
    w_own = []
    for part, ref in enumerate((w_query, w_key, w_value)):
        w_own.append(
            pltpu.make_async_copy(
                ref, wqkv.at[s, gx_rows, part * LANES : (part + 1) * LANES], lsem.at[2 + part]
            )
        )
    w_own.append(pltpu.make_async_copy(w_out, wo.at[s, :, gx_lanes], lsem.at[5]))
    w_own.append(pltpu.make_async_copy(w_up, wup.at[s, gx_rows, :], lsem.at[6]))
    w_own.append(pltpu.make_async_copy(w_down, wdn.at[s, :, gx_lanes], lsem.at[7]))
    for copy in own + vec_own + w_own:
        copy.start()

    pl.semaphore_wait(barrier, 29)

    for device in gy_peers:
        put(images.at[s], xg.at[0, :, mine], gy_send.at[K_X, 0], gy_recv.at[K_X, 0], device)
    for copy in vec_own:
        copy.wait()
    for near, group in ((0, gy_peers), (1, far_gy)):
        for device in group:
            block = vec.at[s, :, :, mine]
            put(block, block, vec_send.at[near], vec_recv.at[near], device)
    for copy in w_own:
        copy.wait()
    own[0].wait()
    own[1].wait()

    def w_block(group):
        if group == 0:
            return wqkv.at[s, gx_rows, :]
        if group == 1:
            return wo.at[s, :, gx_lanes]
        if group == 2:
            return wup.at[s, gx_rows, :]
        return wdn.at[s, :, gx_lanes]

    def send_weights(groups):
        for group in groups:
            block = w_block(group)
            for near, peers in ((0, gx_peers), (1, far_gx)):
                for device in peers:
                    put(block, block, w_send.at[group, near], w_recv.at[group, s], device)

    def wait_weights(group, l):
        if group == 0:
            seven, one = wqkv.at[l, 0:896, :], wqkv.at[l, 0:LANES, :]
        elif group == 1:
            seven, one = wo.at[l, :, 0:896], wo.at[l, :, 0:LANES]
        elif group == 2:
            seven, one = wup.at[l, 0:896, :], wup.at[l, 0:LANES, :]
        else:
            seven, one = wdn.at[l, :, 0:896], wdn.at[l, :, 0:LANES]
        whole = (wqkv, wo, wup, wdn)[group].at[l]

        @pl.when(l == s)
        def _():
            wait_bytes(seven, w_recv.at[group, l])

        @pl.when(l != s)
        def _():
            wait_bytes(whole, w_recv.at[group, l])

    @pl.when(s == 0)
    def _():
        send_weights((0, 1, 2, 3))

    def gather_gy(buffer, kind, l):
        block = buffer.at[l, :, mine]
        for device in gy_peers:
            put(block, block, gy_send.at[kind, l], gy_recv.at[kind, l], device)

    def wait_gather(buffer, kind, l):
        wait_bytes(buffer.at[l, :, 0:896], gy_recv.at[kind, l])

    slot_of = {K_O: 0, K_D: 1, K_N2: 2, K_N1: 3}

    def scatter_gy(partial, kind, l):
        slot = slot_of[kind]
        stage[slot, l] = partial.astype(BF)
        for _, _, peer in gy_peers:
            put(
                stage.at[slot, l, :, lanes(peer)],
                rsb.at[slot, l, gy],
                gy_send.at[kind, l],
                gy_recv.at[kind, l],
                (s, gx, peer),
            )
        rsb[slot, l, gy] = stage[slot, l, :, mine]

    def wait_scatter(kind, l):
        slot = slot_of[kind]
        wait_bytes(rsb.at[slot, l, 0:7], gy_recv.at[kind, l])
        total = rsb[slot, l, 0].astype(F32)
        for source in range(1, 8):
            total = total + rsb[slot, l, source].astype(F32)
        return total

    lane_id = lax.broadcasted_iota(jnp.int32, (TOK, LANES), 1)
    low_half = lane_id < 64
    head_mask = [low_half.astype(F32).astype(BF), (lane_id >= 64).astype(F32).astype(BF)]

    def two_heads(block):
        return jnp.concatenate([block * head_mask[0], block * head_mask[1]], axis=0)

    def join_heads(both):
        return jnp.where(low_half, both[:TOK], both[TOK:])

    def masked_lanes(low, count, value, height):
        ids = lax.broadcasted_iota(jnp.int32, (height, LANES), 1)
        return jnp.where((ids >= low) & (ids < low + count), value, 0.0).astype(BF)

    key_ok = lax.broadcasted_iota(jnp.int32, (ROWS, 640), 1) < SEQ

    def norm_rows(values, gain_row, shift_row, which, l):
        center = values - jnp.mean(values, axis=-1, keepdims=True)
        spread = jnp.mean(center * center, axis=-1, keepdims=True)
        scale = lax.rsqrt(spread + EPS)
        xhat = center * scale
        unit[which, l] = xhat
        rstd[which, l] = jnp.broadcast_to(scale, (ROWS, LANES))
        norm[which, l] = (xhat * vec[l, gain_row] + vec[l, shift_row]).astype(BF)

    res[...] = xg[0, :, mine].astype(F32)
    wait_bytes(vec.at[s, :, :, 0:896], vec_recv.at[0])
    wait_bytes(vec.at[other], vec_recv.at[1])

    def forward(l, carry):
        wait_gather(xg, K_X, l)
        norm_rows(xg[l].astype(F32), V_AG, V_AS, 0, l)
        wait_weights(0, l)
        qkv = dot_nn(norm[0, l], wqkv[l])
        key = qkv[:, LANES : 2 * LANES].astype(BF)
        value = (qkv[:, 2 * LANES :] + vec[l, V_BV, :, mine]).astype(BF)
        query = (qkv[:, :LANES] + vec[l, V_BQ, :, mine]).astype(BF) * jnp.asarray(0.125, BF)
        for c in range(2):
            kv[l, 0, c, gx] = key[c * TOK : (c + 1) * TOK]
            kv[l, 1, c, gx] = value[c * TOK : (c + 1) * TOK]
            qg[l, c, gx] = query[c * TOK : (c + 1) * TOK]
        for device in gx_peers:
            block = kv.at[l, :, :, gx]
            put(block, block, kv_send.at[0, l], kv_recv.at[0, l], device)
        for device in gx_peers:
            block = qg.at[l, :, gx]
            put(block, block, kv_send.at[1, l], kv_recv.at[1, l], device)

        @pl.when((s == 1) & (l == 0))
        def _():
            send_weights((0, 1, 2, 3))

        wait_bytes(kv.at[l, :, :, 0:7], kv_recv.at[0, l])
        for c in range(2):
            all_keys = kv[l, 0, c].reshape(640, LANES)
            all_values = kv[l, 1, c].reshape(640, LANES)
            scores = dot_nt(two_heads(qg[l, c, gx]), all_keys)
            scores = jnp.where(key_ok, scores, NEG)
            highest = jnp.max(scores, axis=-1, keepdims=True)
            exponent = jnp.exp(scores - highest)
            summed = jnp.sum(exponent, axis=-1, keepdims=True)
            full = exponent / summed
            weights = full.astype(BF)
            rest[c] = (full - weights.astype(F32)).astype(BF)
            mixed = join_heads(dot_nn(weights, all_values))
            attn_f[l, c * TOK : (c + 1) * TOK] = mixed
            attn_b[l, c * TOK : (c + 1) * TOK] = mixed.astype(BF)
            logs = highest + jnp.log(summed)
            line = jnp.zeros((TOK, LANES), F32)
            for head in range(2):
                for at, part in enumerate(three_parts(logs[head * TOK : (head + 1) * TOK])):
                    line = jnp.where(lane_id == head * 3 + at, part, line)
            aux[l, c * TOK : (c + 1) * TOK] = line
        wait_weights(1, l)
        scatter_gy(dot_nn(attn_b[l], wo[l]), K_O, l)
        for c in range(2):
            all_values = kv[l, 1, c].reshape(640, LANES)
            attn_f[l, c * TOK : (c + 1) * TOK] += join_heads(dot_nn(rest[c], all_values))
        middle = res[...] + wait_scatter(K_O, l) + vec[l, V_BO, :, mine]
        mid[...] = middle
        mg[l, :, mine] = middle.astype(BF)
        gather_gy(mg, K_M, l)
        wait_gather(mg, K_M, l)
        norm_rows(mg[l].astype(F32), V_MG, V_MS, 1, l)
        wait_weights(2, l)
        bias = jnp.concatenate([vec[l, V_BU + part, :, mine] for part in range(4)], axis=1)
        pre_act = dot_nn(norm[1, l], wup[l]) + bias
        gate = 0.5 * (1.0 + lax.erf(pre_act * 0.7071067811865476))
        hid[l] = (pre_act * gate).astype(BF)
        wait_weights(3, l)
        scatter_gy(dot_nn(hid[l], wdn[l]), K_D, l)
        pre[l] = gate + pre_act * jnp.exp(-0.5 * pre_act * pre_act) * 0.3989422804014327
        output = (mid[...] + wait_scatter(K_D, l) + vec[l, V_BD, :, mine]).astype(BF)
        ybuf[l] = output
        res[...] = output.astype(F32)

        @pl.when(l == 0)
        def _():
            xg[1, :, mine] = output
            gather_gy(xg, K_X, 1)

        @pl.when(l == s)
        def _():
            pltpu.make_async_copy(ybuf.at[l], act_o.at[s], a_recv.at[0]).start()

        @pl.when(l != s)
        def _():
            put(ybuf.at[l], act_o.at[s], a_send.at[0], a_recv.at[0], (other, gx, gy))

        return carry

    lax.fori_loop(0, 2, forward, 0)

    row_id = lax.broadcasted_iota(jnp.int32, (ROWS, LANES), 0)
    image_id = (row_id >= TOK).astype(jnp.int32)
    position = row_id - image_id * TOK + gx * TOK
    live = ((image_id < counts[s]) & (position < SEQ)).astype(F32)
    gcur[...] = cot[...].astype(F32) * live

    def send_grads(groups, l):
        for group in groups:
            for j in range(8):
                k = lax.rem(gx + j, 8)
                if group == 0:
                    src = s_qkv.at[l, lanes(k), :]
                elif group == 1:
                    src = s_wo.at[l, :, lanes(k)]
                elif group == 2:
                    src = s_up.at[l, lanes(k), :]
                elif group == 3:
                    src = s_dn.at[l, :, lanes(k)]
                else:
                    src = s_vec.at[l]
                dst = (r_qkv, r_wo, r_up, r_dn, r_vec)[group].at[s * 8 + gx]
                if j == 0:

                    @pl.when(l == s)
                    def _(src=src, dst=dst, group=group):
                        pltpu.make_async_copy(src, dst, g_recv.at[group]).start()

                    @pl.when(l != s)
                    def _(src=src, dst=dst, group=group, k=k):
                        put(src, dst, g_send.at[group, l], g_recv.at[group], (l, k, gy))

                else:
                    put(src, dst, g_send.at[group, l], g_recv.at[group], (l, k, gy))

    def send_stats(first, second, which, l):
        ids = lax.broadcasted_iota(jnp.int32, (ROWS, LANES), 1)
        both = jnp.where(ids == 0, first, jnp.where(ids == 1, second, 0.0))
        both = jnp.concatenate([both, jnp.zeros((256 - ROWS, LANES), F32)], axis=0)
        stat[which, l, gy] = both.T[:8]
        for device in gy_peers:
            block = stat.at[which, l, gy]
            put(block, block, st_send.at[which, l], st_recv.at[which, l], device)

    def wait_stats(which, l):
        wait_bytes(stat.at[which, l, 0:7], st_recv.at[which, l])
        total = stat[which, l, 0]
        for source in range(1, 8):
            total = total + stat[which, l, source]
        total = jnp.concatenate([total, jnp.zeros((LANES - 8, 256), F32)], axis=0).T
        return total[:ROWS, 0:1], total[:ROWS, 1:2]

    def norm_back_send(partial, which, gain_row, kind, l):
        scatter_gy(partial, kind, l)
        weighted = partial * vec[l, gain_row]
        first = jnp.sum(weighted, axis=-1, keepdims=True)
        second = jnp.sum(weighted * unit[which, l], axis=-1, keepdims=True)
        send_stats(first, second, which, l)

    def norm_back_take(which, gain_row, kind, l, gain_slot, shift_slot):
        grad = wait_scatter(kind, l)
        first, second = wait_stats(which, l)
        xhat = unit[which, l, :, mine]
        vgrad[gain_slot] = row_sum(grad * xhat)
        vgrad[shift_slot] = row_sum(grad)
        inner = grad * vec[l, gain_row, :, mine]
        return rstd[which, l] * (
            inner - first * (1.0 / WIDE) - xhat * (second * (1.0 / WIDE))
        )

    def backward(step, carry):
        l = 1 - step
        grad_out = gcur[...]
        gg[l, :, mine] = grad_out.astype(BF)
        gather_gy(gg, K_G, l)
        vgrad[V_BD] = row_sum(grad_out)
        wait_gather(gg, K_G, l)
        grad_hid = dot_nt(gg[l], wdn[l])
        grad_pre32 = grad_hid * pre[l]
        grad_pre = grad_pre32.astype(BF)
        norm_back_send(dot_nt(grad_pre, wup[l]), 1, V_MG, K_N2, l)
        up_sum = row_sum(grad_pre.astype(F32))
        for part in range(4):
            vgrad[V_BU + part] = up_sum[:, part * LANES : (part + 1) * LANES]
        s_dn[l] = dot_tn(hid[l], gg[l]).astype(BF)
        send_grads((3,), l)
        s_up[l] = dot_tn(norm[1, l], grad_pre).astype(BF)
        send_grads((2,), l)
        grad_mid = gcur[...] + norm_back_take(1, V_MG, K_N2, l, V_MG, V_MS)
        gmid[...] = grad_mid
        gmg[l, :, mine] = grad_mid.astype(BF)
        gather_gy(gmg, K_GM, l)
        vgrad[V_BO] = row_sum(grad_mid)
        wait_gather(gmg, K_GM, l)
        grad_mixed = dot_nt(gmg[l], wo[l]).astype(BF)
        grad_mixed32 = grad_mixed.astype(F32)
        for c in range(2):
            part32 = grad_mixed32[c * TOK : (c + 1) * TOK]
            product = part32 * attn_f[l, c * TOK : (c + 1) * TOK]
            line = aux[l, c * TOK : (c + 1) * TOK]
            for head in range(2):
                picked = jnp.where(low_half == (head == 0), product, 0.0)
                delta = jnp.sum(picked, axis=-1, keepdims=True)
                for at, part in enumerate(three_parts(delta)):
                    line = jnp.where(lane_id == 6 + head * 3 + at, part, line)
            dog[l, c, gx, :, 0:LANES] = grad_mixed[c * TOK : (c + 1) * TOK]
            dog[l, c, gx, :, LANES:] = line.astype(BF)
        for device in gx_peers:
            block = dog.at[l, :, gx]
            put(block, block, do_send.at[l], do_recv.at[l], device)
        s_wo[l] = dot_tn(attn_b[l], gmg[l]).astype(BF)
        send_grads((1,), l)

        @pl.when(l == 1)
        def _():
            wait_bytes(qg.at[0, :, 0:7], kv_recv.at[1, 0])
            wait_bytes(qg.at[1, :, 0:7], kv_recv.at[1, 1])

        wait_bytes(dog.at[l, :, 0:7], do_recv.at[l])
        key_side = masked_lanes(0, 6, -1.0, 640)
        value_side = masked_lanes(6, 6, -1.0, 640)
        row_ids = lax.broadcasted_iota(jnp.int32, (ROWS, 640), 0)
        key_pos = jnp.where(row_ids >= TOK, row_ids - TOK, row_ids) + gx * TOK
        own_ok = key_pos < SEQ
        for c in range(2):
            all_keys = kv[l, 0, c].reshape(640, LANES)
            all_values = kv[l, 1, c].reshape(640, LANES)
            all_query = qg[l, c].reshape(640, LANES)
            all_grads = dog[l, c].reshape(640, 2 * LANES)
            all_aux = all_grads[:, LANES:]
            all_mixed = all_grads[:, :LANES]
            my_aux = dog[l, c, gx, :, LANES:]
            my_log = jnp.concatenate(
                [my_aux * masked_lanes(0, 3, 1.0, TOK), my_aux * masked_lanes(3, 3, 1.0, TOK)],
                axis=0,
            )
            my_delta = jnp.concatenate(
                [my_aux * masked_lanes(6, 3, 1.0, TOK), my_aux * masked_lanes(9, 3, 1.0, TOK)],
                axis=0,
            )
            my_query = jnp.concatenate([two_heads(qg[l, c, gx]), my_log], axis=1)
            my_mixed = jnp.concatenate([two_heads(dog[l, c, gx, :, 0:LANES]), my_delta], axis=1)
            scores = dot_nt(my_query, jnp.concatenate([all_keys, key_side], axis=1))
            weights = jnp.exp(jnp.where(key_ok, scores, NEG))
            inner = dot_nt(my_mixed, jnp.concatenate([all_values, value_side], axis=1))
            grad_scores = (weights * inner).astype(BF)
            grad_query = join_heads(dot_nn(grad_scores, all_keys)) * 0.125
            owna[c * TOK : (c + 1) * TOK, 0:LANES] = grad_query.astype(BF)

            key_log = jnp.concatenate(
                [masked_lanes(0, 3, -1.0, TOK), masked_lanes(3, 3, -1.0, TOK)], axis=0
            )
            key_delta = jnp.concatenate(
                [masked_lanes(6, 3, -1.0, TOK), masked_lanes(9, 3, -1.0, TOK)], axis=0
            )
            my_key = jnp.concatenate([two_heads(kv[l, 0, c, gx]), key_log], axis=1)
            my_value = jnp.concatenate([two_heads(kv[l, 1, c, gx]), key_delta], axis=1)
            scores = dot_nt(my_key, jnp.concatenate([all_query, all_aux], axis=1))
            weights = jnp.exp(jnp.where(own_ok, scores, NEG))
            inner = dot_nt(my_value, all_grads)
            grad_scores = (weights * inner).astype(BF)
            grad_key = join_heads(dot_nn(grad_scores, all_query))
            grad_value = join_heads(dot_nn(weights.astype(BF), all_mixed))
            owna[c * TOK : (c + 1) * TOK, LANES : 2 * LANES] = grad_key.astype(BF)
            owna[c * TOK : (c + 1) * TOK, 2 * LANES :] = grad_value.astype(BF)
        grad_qkv = owna[...]
        norm_back_send(dot_nt(grad_qkv, wqkv[l]), 0, V_AG, K_N1, l)
        s_qkv[l] = dot_tn(norm[0, l], grad_qkv).astype(BF)
        send_grads((0,), l)
        bias_sum = row_sum(grad_qkv.astype(F32))
        vgrad[V_BQ] = bias_sum[:, :LANES]
        vgrad[V_BV] = bias_sum[:, 2 * LANES :]
        grad_in = gmid[...] + norm_back_take(0, V_AG, K_N1, l, V_AG, V_AS)
        igbuf[l] = grad_in
        gcur[...] = grad_in.astype(BF).astype(F32)
        s_vec[l] = vgrad[...]
        send_grads((4,), l)

        @pl.when(l == s)
        def _():
            pltpu.make_async_copy(igbuf.at[l], ig_o.at[s], i_recv.at[0]).start()

        @pl.when(l != s)
        def _():
            put(igbuf.at[l], ig_o.at[s], i_send.at[0], i_recv.at[0], (other, gx, gy))

        return carry

    lax.fori_loop(0, 2, backward, 0)

    def sum_of(ref):
        total = ref[0].astype(F32)
        for source in range(1, 16):
            total = total + ref[source].astype(F32)
        return total

    wait_bytes(r_dn, g_recv.at[3])
    g_w_down[...] = sum_of(r_dn)
    wait_bytes(r_up, g_recv.at[2])
    g_w_up[...] = sum_of(r_up)
    wait_bytes(r_wo, g_recv.at[1])
    g_w_out[...] = sum_of(r_wo)
    wait_bytes(r_qkv, g_recv.at[0])
    total = sum_of(r_qkv)
    g_w_query[...] = total[:, :LANES]
    g_w_key[...] = total[:, LANES : 2 * LANES]
    g_w_value[...] = total[:, 2 * LANES :]
    wait_bytes(r_vec, g_recv.at[4])
    total = sum_of(r_vec)
    g_attn_gain[...] = total[V_AG]
    g_attn_shift[...] = total[V_AS]
    g_mlp_gain[...] = total[V_MG]
    g_mlp_shift[...] = total[V_MS]
    g_b_query[...] = total[V_BQ]
    g_b_value[...] = total[V_BV]
    g_b_out[...] = total[V_BO]
    g_b_down[...] = total[V_BD]
    for part in range(4):
        g_b_up[:, part * LANES : (part + 1) * LANES] = total[V_BU + part]
    wait_bytes(act_o, a_recv.at[0])
    wait_bytes(ig_o, i_recv.at[0])

    wait_bytes(ybuf.at[0], a_send.at[0])
    wait_bytes(igbuf.at[0], i_send.at[0])
    wait_bytes(vec.at[s, :, :, 0:896], vec_send.at[0])
    wait_bytes(vec.at[s], vec_send.at[1])
    wholes = (wqkv, wo, wup, wdn)
    sevens = (
        wqkv.at[0, 0:896, :],
        wo.at[0, :, 0:896],
        wup.at[0, 0:896, :],
        wdn.at[0, :, 0:896],
    )
    for group in range(4):
        wait_bytes(sevens[group], w_send.at[group, 0])
        wait_bytes(wholes[group].at[0], w_send.at[group, 1])
    received = (r_qkv, r_wo, r_up, r_dn, r_vec)
    for l in range(2):
        for kind, buffer in ((K_X, xg), (K_M, mg), (K_G, gg), (K_GM, gmg)):
            wait_bytes(buffer.at[l, :, 0:896], gy_send.at[kind, l])
        for kind, slot in slot_of.items():
            wait_bytes(rsb.at[slot, l, 0:7], gy_send.at[kind, l])
        for which in range(2):
            wait_bytes(stat.at[which, l, 0:7], st_send.at[which, l])
        wait_bytes(kv.at[l, :, :, 0:7], kv_send.at[0, l])
        wait_bytes(qg.at[l, :, 0:7], kv_send.at[1, l])
        wait_bytes(dog.at[l, :, 0:7], do_send.at[l])

        @pl.when(s == l)
        def _(l=l):
            for group in range(5):
                wait_bytes(received[group].at[0:7], g_send.at[group, l])

        @pl.when(s != l)
        def _(l=l):
            for group in range(5):
                wait_bytes(received[group].at[0:8], g_send.at[group, l])


def local(
    images, counts, attn_gain, attn_shift, w_query, b_query, w_key, w_value, b_value, w_out,
    b_out, mlp_gain, mlp_shift, w_up, b_up, w_down, b_down, cotangent,
):
    anywhere = pl.BlockSpec(memory_space=pl.ANY)
    in_vmem = pl.BlockSpec(memory_space=pltpu.VMEM)
    in_smem = pl.BlockSpec(memory_space=pltpu.SMEM)
    in_specs = [anywhere, in_smem] + [anywhere] * 16
    row = jax.ShapeDtypeStruct((1, LANES), F32)
    square = jax.ShapeDtypeStruct((LANES, LANES), F32)
    out_shape = [
        jax.ShapeDtypeStruct((2, ROWS, LANES), BF),
        jax.ShapeDtypeStruct((2, ROWS, LANES), F32),
        row, row, square, row, square, square, row, square, row, row, row,
        jax.ShapeDtypeStruct((LANES, 512), F32),
        jax.ShapeDtypeStruct((1, 512), F32),
        jax.ShapeDtypeStruct((512, LANES), F32),
        row,
    ]
    vmem = pltpu.VMEM
    scratch = [
        vmem((2, 12, 1, WIDE), F32),
        vmem((ROWS, LANES), BF),
        vmem((2, WIDE, 384), BF),
        vmem((2, LANES, WIDE), BF),
        vmem((2, WIDE, 512), BF),
        vmem((2, 512, WIDE), BF),
        vmem((2, ROWS, WIDE), BF),
        vmem((2, ROWS, WIDE), BF),
        vmem((2, ROWS, WIDE), BF),
        vmem((2, ROWS, WIDE), BF),
        vmem((2, 2, ROWS, WIDE), BF),
        vmem((2, 2, ROWS, WIDE), F32),
        vmem((2, 2, ROWS, LANES), F32),
        vmem((ROWS, LANES), F32),
        vmem((ROWS, LANES), F32),
        vmem((ROWS, LANES), F32),
        vmem((ROWS, LANES), F32),
        vmem((4, 2, ROWS, WIDE), BF),
        vmem((4, 2, 8, ROWS, LANES), BF),
        vmem((2, 2, 8, 8, 256), F32),
        vmem((2, 2, 2, 8, TOK, LANES), BF),
        vmem((2, 2, 8, TOK, LANES), BF),
        vmem((2, 2, 8, TOK, 2 * LANES), BF),
        vmem((ROWS, 384), BF),
        vmem((2, ROWS, LANES), F32),
        vmem((2, ROWS, LANES), BF),
        vmem((2, ROWS, LANES), F32),
        vmem((2, ROWS, 512), BF),
        vmem((2, ROWS, 512), F32),
        vmem((2, ROWS, 640), BF),
        vmem((2, ROWS, LANES), BF),
        vmem((2, ROWS, LANES), F32),
        vmem((2, 512, WIDE), BF),
        vmem((2, WIDE, 512), BF),
        vmem((2, LANES, WIDE), BF),
        vmem((2, WIDE, 384), BF),
        vmem((2, 12, 1, LANES), F32),
        vmem((16, 512, LANES), BF),
        vmem((16, LANES, 512), BF),
        vmem((16, LANES, LANES), BF),
        vmem((16, LANES, 384), BF),
        vmem((16, 12, 1, LANES), F32),
        vmem((12, 1, LANES), F32),
        pltpu.SemaphoreType.DMA((20,)),
        pltpu.SemaphoreType.DMA((8, 2)),
        pltpu.SemaphoreType.DMA((8, 2)),
        pltpu.SemaphoreType.DMA((2, 2)),
        pltpu.SemaphoreType.DMA((2, 2)),
        pltpu.SemaphoreType.DMA((2, 2)),
        pltpu.SemaphoreType.DMA((2, 2)),
        pltpu.SemaphoreType.DMA((2,)),
        pltpu.SemaphoreType.DMA((2,)),
        pltpu.SemaphoreType.DMA((2,)),
        pltpu.SemaphoreType.DMA((2,)),
        pltpu.SemaphoreType.DMA((4, 2)),
        pltpu.SemaphoreType.DMA((4, 2)),
        pltpu.SemaphoreType.DMA((5, 2)),
        pltpu.SemaphoreType.DMA((5,)),
        pltpu.SemaphoreType.DMA((1,)),
        pltpu.SemaphoreType.DMA((1,)),
        pltpu.SemaphoreType.DMA((1,)),
        pltpu.SemaphoreType.DMA((1,)),
    ]
    outs = pl.pallas_call(
        kernel,
        out_shape=out_shape,
        in_specs=in_specs,
        out_specs=[in_vmem] * 17,
        scratch_shapes=scratch,
        compiler_params=pltpu.CompilerParams(
            collective_id=0, has_side_effects=True, vmem_limit_bytes=58 * 1024 * 1024
        ),
        cost_estimate=pl.CostEstimate(
            flops=4_000_000_000, bytes_accessed=8_000_000, transcendentals=4_000_000
        ),
        name="two_sections",
    )(
        images.reshape(2, ROWS, LANES), counts, attn_gain, attn_shift, w_query[0], b_query,
        w_key[0], w_value[0], b_value, w_out[0], b_out, mlp_gain, mlp_shift, w_up[0], b_up,
        w_down[0], b_down, cotangent.reshape(2, ROWS, LANES),
    )
    outs = list(outs)
    shape = (1,) + images.shape
    outs[0] = outs[0].reshape(shape)
    outs[1] = outs[1].reshape(shape)
    for index in (4, 6, 7, 9, 13, 15):
        outs[index] = outs[index][None]
    return tuple(outs)


def solution(mesh):
    vector = P("section", "gy")
    in_block = P("section", "gx", "gy")
    out_block = P("section", "gy", "gx")
    rows = P(None, None, "gx", "gy")
    in_specs = (
        rows, P(), vector, vector, in_block, vector, in_block, in_block, vector, out_block,
        vector, vector, vector, in_block, vector, out_block, vector, rows,
    )
    results = P("section", None, None, "gx", "gy")
    out_specs = (
        results, results, vector, vector, in_block, vector, in_block, in_block, vector,
        out_block, vector, vector, vector, in_block, vector, out_block, vector,
    )
    return jax.shard_map(local, mesh=mesh, in_specs=in_specs, out_specs=out_specs, check_vma=False)
```

```python
import jax
import jax.numpy as jnp
from jax import lax
from jax.experimental import pallas as pl
from jax.experimental.pallas import tpu as pltpu
from jax.sharding import PartitionSpec as P

BF = jnp.bfloat16
F32 = jnp.float32
SEQ = 577
EPS = 1e-06
NEG = -1e30
ROWS = 160
TOK = 80
LANES = 128
WIDE = 1024
MESH = pl.DeviceIdType.MESH

K_X, K_O, K_M, K_D, K_G, K_N2, K_GM, K_N1 = range(8)
V_AG, V_AS, V_MG, V_MS, V_BQ, V_BV, V_BO, V_BD, V_BU = range(9)


def dot_nn(a, b):
    return lax.dot_general(a, b, (((1,), (0,)), ((), ())), preferred_element_type=F32)


def dot_nt(a, b):
    return lax.dot_general(a, b, (((1,), (1,)), ((), ())), preferred_element_type=F32)


def dot_tn(a, b):
    return lax.dot_general(a, b, (((0,), (0,)), ((), ())), preferred_element_type=F32)


def lanes(index):
    return pl.ds(pl.multiple_of(index * LANES, LANES), LANES)


def wait_bytes(ref, sem):
    pltpu.make_async_copy(ref, ref, sem).wait()


def put(src, dst, send_sem, recv_sem, device):
    pltpu.make_async_remote_copy(
        src_ref=src,
        dst_ref=dst,
        send_sem=send_sem,
        recv_sem=recv_sem,
        device_id=device,
        device_id_type=MESH,
    ).start()


def image_rows(c):
    return pl.ds(c * TOK, TOK)


def row_sum(values):
    return jnp.sum(values, axis=0, keepdims=True)


def three_parts(values):
    high = values.astype(BF).astype(F32)
    rest = values - high
    mid = rest.astype(BF).astype(F32)
    return high, mid, rest - mid


def kernel(
    images, counts, attn_gain, attn_shift, w_query, b_query, w_key, w_value, b_value, w_out,
    b_out, mlp_gain, mlp_shift, w_up, b_up, w_down, b_down, cotangent,
    act_o, ig_o, g_attn_gain, g_attn_shift, g_w_query, g_b_query, g_w_key, g_w_value, g_b_value,
    g_w_out, g_b_out, g_mlp_gain, g_mlp_shift, g_w_up, g_b_up, g_w_down, g_b_down,
    vec, cot, wqkv, wo, wup, wdn,
    xg, mg, gg, gmg, norm, unit, rstd, res, mid, gcur, gmid,
    stage, rsb, stat, kv, qg, dog, owna, attn_f, attn_b, aux, hid, pre,
    grad_pre, ybuf, igbuf, s_vec, r_vec, vgrad,
    lsem, gy_send, gy_recv, st_send, st_recv, kv_send, kv_recv, do_send, do_recv,
    vec_send, vec_recv, wa1_send, wa1_recv, wa2_send, wa2_recv, wb1_send, wb1_recv, wb2_send,
    wb2_recv, ga1_send, ga1_recv, ga2_send, ga2_recv, gb1_send, gb1_recv, gb2_send, gb2_recv,
    v_send, v_recv, a_send, a_recv, i_send, i_recv, *grad_refs,
):
    staged, ra1, pa, ra2, rb1, pb, rb2 = [grad_refs[4 * n : 4 * n + 4] for n in range(7)]
    weights_at = (wqkv, wo, wup, wdn)
    s = lax.axis_index("section")
    gx = lax.axis_index("gx")
    gy = lax.axis_index("gy")
    other = 1 - s
    mine = lanes(gy)
    x = gx // 2
    h = lax.rem(gx, 2)
    y_slot = h * 2 + s

    barrier = pltpu.get_barrier_semaphore()

    def greet(device):
        pl.semaphore_signal(barrier, inc=1, device_id=device, device_id_type=MESH)

    gy_peers = [(s, gx, lax.rem(gy + k, 8)) for k in range(1, 8)]
    gx_peers = [(s, lax.rem(gx + k, 8), gy) for k in range(1, 8)]
    far_gx = [(other, lax.rem(gx + k, 8), gy) for k in range(8)]
    far_gy = [(other, gx, lax.rem(gy + k, 8)) for k in range(8)]
    x_peers = [(s, lax.rem(x + k, 4) * 2 + h, gy) for k in range(1, 4)]
    y_peers = [(s, x * 2 + 1 - h, gy), (other, gx, gy), (other, x * 2 + 1 - h, gy)]
    for device in gy_peers + gx_peers + far_gx + far_gy[1:]:
        greet(device)

    own = [pltpu.make_async_copy(images.at[s], xg.at[0, :, mine], lsem.at[0])]
    own.append(pltpu.make_async_copy(cotangent.at[s], cot, lsem.at[1]))
    rows = [attn_gain, attn_shift, mlp_gain, mlp_shift, b_query, b_value, b_out, b_down]
    vec_own = []
    for row, ref in enumerate(rows):
        vec_own.append(pltpu.make_async_copy(ref, vec.at[s, row, :, mine], lsem.at[8 + row]))
    for part in range(4):
        vec_own.append(
            pltpu.make_async_copy(
                b_up.at[:, part * LANES : (part + 1) * LANES],
                vec.at[s, V_BU + part, :, mine],
                lsem.at[16 + part],
            )
        )
    w_own = []
    for part, ref in enumerate((w_query, w_key, w_value)):
        w_own.append(
            pltpu.make_async_copy(
                ref, wqkv.at[s, x, h, :, part * LANES : (part + 1) * LANES], lsem.at[2 + part]
            )
        )
    w_own.append(pltpu.make_async_copy(w_out, wo.at[s, x, h], lsem.at[5]))
    w_own.append(pltpu.make_async_copy(w_up, wup.at[s, x, h], lsem.at[6]))
    w_own.append(pltpu.make_async_copy(w_down, wdn.at[s, x, h], lsem.at[7]))
    for copy in own + vec_own + w_own:
        copy.start()

    pl.semaphore_wait(barrier, 29)

    for c in range(2):
        for device in gy_peers:
            put(
                images.at[s, image_rows(c)],
                xg.at[0, image_rows(c), mine],
                gy_send.at[K_X, 0, c],
                gy_recv.at[K_X, 0, c],
                device,
            )
    for copy in vec_own:
        copy.wait()
    for near, group in ((0, gy_peers), (1, far_gy)):
        for device in group:
            block = vec.at[s, :, :, mine]
            put(block, block, vec_send.at[near], vec_recv.at[near], device)
    for copy in w_own:
        copy.wait()
    own[0].wait()
    own[1].wait()

    half_rows = (64, 64, 64, 256)

    def halves(group):
        return pl.ds(0, half_rows[group]), pl.ds(half_rows[group], half_rows[group])

    def spread_own(groups):
        for group in groups:
            ref = weights_at[group]
            first, second = halves(group)
            block = ref.at[s, x, h, first]
            for device in x_peers:
                put(block, block, wa1_send.at[group], wa1_recv.at[group], device)
            block = ref.at[s, x, h, second]
            for device in y_peers:
                put(block, block, wb1_send.at[group], wb1_recv.at[group, s], device)

    def pass_on(groups, l):
        for group in groups:
            ref = weights_at[group]
            first, second = halves(group)

            @pl.when(l == s)
            def _(ref=ref, first=first, group=group):
                wait_bytes(ref.at[l, 0:3, 0, first], wa1_recv.at[group])
                block = ref.at[s, :, h, first]
                for device in y_peers:
                    put(block, block, wa2_send.at[group], wa2_recv.at[group, s], device)
                wait_bytes(ref.at[l, 0, 0, first], wb1_recv.at[group, l])

            @pl.when(l != s)
            def _(ref=ref, first=first, group=group):
                wait_bytes(ref.at[l, 0, :, first], wb1_recv.at[group, l])

            block = ref.at[l, x, :, second]
            for device in x_peers:
                put(block, block, wb2_send.at[group, l], wb2_recv.at[group, l], device)

    def wait_weights(group, l):
        ref = weights_at[group]
        first, _ = halves(group)

        @pl.when(l == s)
        def _():
            wait_bytes(ref.at[l, :, 0, first], wa2_recv.at[group, l])

        @pl.when(l != s)
        def _():
            wait_bytes(ref.at[l, :, :, first], wa2_recv.at[group, l])

        wait_bytes(ref.at[l, 0:3, :, first], wb2_recv.at[group, l])

    def by_columns(ref, l):
        return jnp.concatenate([ref[l, a, b] for a in range(4) for b in range(2)], axis=1)

    @pl.when(s == 0)
    def _():
        spread_own((0, 1, 2, 3))

    def gather_gy(buffer, kind, l, c):
        block = buffer.at[l, image_rows(c), mine]
        for device in gy_peers:
            put(block, block, gy_send.at[kind, l, c], gy_recv.at[kind, l, c], device)

    def wait_gather(buffer, kind, l, c):
        wait_bytes(buffer.at[l, image_rows(c), 0:896], gy_recv.at[kind, l, c])

    slot_of = {K_O: 0, K_D: 1, K_N2: 2, K_N1: 3}

    def scatter_gy(partial, kind, l, c):
        slot = slot_of[kind]
        stage[slot, l, image_rows(c)] = partial.astype(BF)
        for _, _, peer in gy_peers:
            put(
                stage.at[slot, l, image_rows(c), lanes(peer)],
                rsb.at[slot, l, c, gy],
                gy_send.at[kind, l, c],
                gy_recv.at[kind, l, c],
                (s, gx, peer),
            )
        rsb[slot, l, c, gy] = stage[slot, l, image_rows(c), mine]

    def wait_scatter(kind, l, c):
        slot = slot_of[kind]
        wait_bytes(rsb.at[slot, l, c, 0:7], gy_recv.at[kind, l, c])
        total = rsb[slot, l, c, 0].astype(F32)
        for source in range(1, 8):
            total = total + rsb[slot, l, c, source].astype(F32)
        return total

    lane_id = lax.broadcasted_iota(jnp.int32, (TOK, LANES), 1)
    low_half = lane_id < 64
    head_mask = [low_half.astype(F32).astype(BF), (lane_id >= 64).astype(F32).astype(BF)]

    def two_heads(block):
        return jnp.concatenate([block * head_mask[0], block * head_mask[1]], axis=0)

    def join_heads(both):
        return jnp.where(low_half, both[:TOK], both[TOK:])

    def masked_lanes(low, count, value, height):
        ids = lax.broadcasted_iota(jnp.int32, (height, LANES), 1)
        return jnp.where((ids >= low) & (ids < low + count), value, 0.0).astype(BF)

    key_ok = lax.broadcasted_iota(jnp.int32, (ROWS, 640), 1) < SEQ

    def norm_rows(values, gain_row, shift_row, which, l, c):
        center = values - jnp.mean(values, axis=-1, keepdims=True)
        spread = jnp.mean(center * center, axis=-1, keepdims=True)
        scale = lax.rsqrt(spread + EPS)
        xhat = center * scale
        unit[which, l, image_rows(c)] = xhat
        rstd[which, l, image_rows(c)] = jnp.broadcast_to(scale, (TOK, LANES))
        normed = (xhat * vec[l, gain_row] + vec[l, shift_row]).astype(BF)
        norm[which, l, image_rows(c)] = normed
        return normed

    pass_on((0,), 0)

    res[...] = xg[0, :, mine].astype(F32)
    wait_bytes(vec.at[s, :, :, 0:896], vec_recv.at[0])
    wait_bytes(vec.at[other], vec_recv.at[1])

    def forward(l, carry):
        for c in range(2):
            wait_gather(xg, K_X, l, c)
            normed = norm_rows(xg[l, image_rows(c)].astype(F32), V_AG, V_AS, 0, l, c)
            if c == 0:
                wait_weights(0, l)
            qkv = dot_nn(normed, wqkv[l].reshape(WIDE, 384))
            kv[l, 0, c, gx] = qkv[:, LANES : 2 * LANES].astype(BF)
            kv[l, 1, c, gx] = (qkv[:, 2 * LANES :] + vec[l, V_BV, :, mine]).astype(BF)
            query = (qkv[:, :LANES] + vec[l, V_BQ, :, mine]).astype(BF)
            qg[l, c, gx] = query * jnp.asarray(0.125, BF)
            for device in gx_peers:
                block = kv.at[l, :, c, gx]
                put(block, block, kv_send.at[0, l, c], kv_recv.at[0, l, c], device)
        for device in gx_peers:
            block = qg.at[l, :, gx]
            put(block, block, kv_send.at[1, l, 0], kv_recv.at[1, l, 0], device)

        @pl.when(l == 0)
        def _():
            pass_on((1, 2, 3), 0)

            @pl.when(s == 1)
            def _():
                spread_own((0, 1, 2, 3))

        for c in range(2):
            wait_bytes(kv.at[l, :, c, 0:7], kv_recv.at[0, l, c])
            all_keys = kv[l, 0, c].reshape(640, LANES)
            all_values = kv[l, 1, c].reshape(640, LANES)
            scores = dot_nt(two_heads(qg[l, c, gx]), all_keys)
            scores = jnp.where(key_ok, scores, NEG)
            highest = jnp.max(scores, axis=-1, keepdims=True)
            exponent = jnp.exp(scores - highest)
            summed = jnp.sum(exponent, axis=-1, keepdims=True)
            full = exponent / summed
            weights = full.astype(BF)
            mixed = join_heads(dot_nn(weights, all_values))
            mixed_low = mixed.astype(BF)
            attn_b[l, image_rows(c)] = mixed_low
            if c == 0:
                wait_weights(1, l)
            scatter_gy(dot_nn(mixed_low, by_columns(wo, l)), K_O, l, c)
            left_out = (full - weights.astype(F32)).astype(BF)
            attn_f[l, image_rows(c)] = mixed + join_heads(dot_nn(left_out, all_values))
            logs = highest + jnp.log(summed)
            line = jnp.zeros((TOK, LANES), F32)
            for head in range(2):
                for at, piece in enumerate(three_parts(logs[head * TOK : (head + 1) * TOK])):
                    line = jnp.where(lane_id == head * 3 + at, piece, line)
            aux[l, image_rows(c)] = line
        for c in range(2):
            middle = res[image_rows(c)] + wait_scatter(K_O, l, c) + vec[l, V_BO, :, mine]
            mid[image_rows(c)] = middle
            mg[l, image_rows(c), mine] = middle.astype(BF)
            gather_gy(mg, K_M, l, c)
        bias = jnp.concatenate([vec[l, V_BU + n, :, mine] for n in range(4)], axis=1)
        for c in range(2):
            wait_gather(mg, K_M, l, c)
            normed = norm_rows(mg[l, image_rows(c)].astype(F32), V_MG, V_MS, 1, l, c)
            if c == 0:
                wait_weights(2, l)
            pre_act = dot_nn(normed, wup[l].reshape(WIDE, 512)) + bias
            gate = 0.5 * (1.0 + lax.erf(pre_act * 0.7071067811865476))
            hidden = (pre_act * gate).astype(BF)
            hid[l, image_rows(c)] = hidden
            if c == 0:
                wait_weights(3, l)
            scatter_gy(dot_nn(hidden, by_columns(wdn, l)), K_D, l, c)
            slope = jnp.exp(-0.5 * pre_act * pre_act) * 0.3989422804014327
            pre[l, image_rows(c)] = gate + pre_act * slope

        @pl.when(l == 0)
        def _():
            pass_on((0, 1, 2, 3), 1)

        for c in range(2):
            output = mid[image_rows(c)] + wait_scatter(K_D, l, c) + vec[l, V_BD, :, mine]
            output = output.astype(BF)
            ybuf[l, image_rows(c)] = output
            res[image_rows(c)] = output.astype(F32)

            @pl.when(l == 0)
            def _(c=c, output=output):
                xg[1, image_rows(c), mine] = output
                gather_gy(xg, K_X, 1, c)

        @pl.when(l == s)
        def _():
            pltpu.make_async_copy(ybuf.at[l], act_o.at[s], a_recv.at[0]).start()

        @pl.when(l != s)
        def _():
            put(ybuf.at[l], act_o.at[s], a_send.at[0], a_recv.at[0], (other, gx, gy))

        return carry

    lax.fori_loop(0, 2, forward, 0)

    row_id = lax.broadcasted_iota(jnp.int32, (ROWS, LANES), 0)
    image_id = (row_id >= TOK).astype(jnp.int32)
    position = row_id - image_id * TOK + gx * TOK
    live = ((image_id < counts[s]) & (position < SEQ)).astype(F32)
    gcur[...] = cot[...].astype(F32) * live

    def reduce_start(groups, l):
        for group in groups:
            first, second = halves(group)
            ref = staged[group]
            for _, peer, _ in x_peers:
                put(
                    ref.at[l, peer // 2, :, first],
                    ra1[group].at[l, x],
                    ga1_send.at[group, l],
                    ga1_recv.at[group, l],
                    (s, peer, gy),
                )
            put(
                ref.at[l, :, 1 - h, second],
                rb1[group].at[y_slot],
                gb1_send.at[group, l],
                gb1_recv.at[group],
                (l, x * 2 + 1 - h, gy),
            )

            @pl.when(l != s)
            def _(ref=ref, second=second, group=group):
                put(
                    ref.at[l, :, h, second],
                    rb1[group].at[y_slot],
                    gb1_send.at[group, l],
                    gb1_recv.at[group],
                    (l, gx, gy),
                )

            ra1[group][l, x] = ref[l, x, :, first]

            @pl.when(l == s)
            def _(ref=ref, second=second, group=group):
                rb1[group][y_slot] = ref[l, :, h, second]

    def four(ref, index=None):
        parts = [(ref[n] if index is None else ref[index, n]).astype(F32) for n in range(4)]
        return (parts[0] + parts[1]) + (parts[2] + parts[3])

    def reduce_turn(groups, l):
        for group in groups:
            wait_bytes(ra1[group].at[l, 0:3], ga1_recv.at[group, l])
            pa[group][l] = four(ra1[group], l).astype(BF)
            put(
                pa[group].at[l, 1 - h],
                ra2[group].at[y_slot],
                ga2_send.at[group, l],
                ga2_recv.at[group],
                (l, x * 2 + 1 - h, gy),
            )

            @pl.when(l != s)
            def _(group=group):
                put(
                    pa[group].at[l, h],
                    ra2[group].at[y_slot],
                    ga2_send.at[group, l],
                    ga2_recv.at[group],
                    (l, gx, gy),
                )

            @pl.when(l == s)
            def _(group=group):
                ra2[group][y_slot] = pa[group][l, h]
                wait_bytes(rb1[group].at[0:3], gb1_recv.at[group])
                pb[group][...] = four(rb1[group]).astype(BF)
                for _, peer, _ in x_peers:
                    put(
                        pb[group].at[peer // 2],
                        rb2[group].at[x],
                        gb2_send.at[group],
                        gb2_recv.at[group],
                        (s, peer, gy),
                    )
                rb2[group][x] = pb[group][x]

    def send_vec(l):
        for j in range(8):
            k = lax.rem(gx + j, 8)
            dst = r_vec.at[s * 8 + gx]
            if j == 0:

                @pl.when(l == s)
                def _():
                    r_vec[s * 8 + gx] = s_vec[l]

                @pl.when(l != s)
                def _(k=k):
                    put(s_vec.at[l], r_vec.at[s * 8 + gx], v_send.at[l], v_recv.at[0], (l, k, gy))

            else:
                put(s_vec.at[l], dst, v_send.at[l], v_recv.at[0], (l, k, gy))

    def send_stats(first, second, which, l, c):
        ids = lax.broadcasted_iota(jnp.int32, (TOK, LANES), 1)
        both = jnp.where(ids == 0, first, jnp.where(ids == 1, second, 0.0))
        both = jnp.concatenate([both, jnp.zeros((LANES - TOK, LANES), F32)], axis=0)
        stat[which, l, c, gy] = both.T[:8]
        for device in gy_peers:
            block = stat.at[which, l, c, gy]
            put(block, block, st_send.at[which, l, c], st_recv.at[which, l, c], device)

    def wait_stats(which, l, c):
        wait_bytes(stat.at[which, l, c, 0:7], st_recv.at[which, l, c])
        total = stat[which, l, c, 0]
        for source in range(1, 8):
            total = total + stat[which, l, c, source]
        total = jnp.concatenate([total, jnp.zeros((LANES - 8, LANES), F32)], axis=0).T
        return total[:TOK, 0:1], total[:TOK, 1:2]

    def norm_back_send(partial, which, gain_row, kind, l, c):
        scatter_gy(partial, kind, l, c)
        weighted = partial * vec[l, gain_row]
        first = jnp.sum(weighted, axis=-1, keepdims=True)
        second = jnp.sum(weighted * unit[which, l, image_rows(c)], axis=-1, keepdims=True)
        send_stats(first, second, which, l, c)

    def add_vec(slot, value, c):
        if c == 0:
            vgrad[slot] = value
        else:
            vgrad[slot] += value

    def norm_back_take(which, gain_row, kind, l, c, gain_slot, shift_slot):
        grad = wait_scatter(kind, l, c)
        first, second = wait_stats(which, l, c)
        xhat = unit[which, l, image_rows(c), mine]
        add_vec(gain_slot, row_sum(grad * xhat), c)
        add_vec(shift_slot, row_sum(grad), c)
        inner = grad * vec[l, gain_row, :, mine]
        return rstd[which, l, image_rows(c)] * (
            inner - first * (1.0 / WIDE) - xhat * (second * (1.0 / WIDE))
        )

    def store_columns(group, grad, l):
        for block in range(8):
            columns = grad[:, block * LANES : (block + 1) * LANES]
            staged[group][l, block // 2, block % 2] = columns.astype(BF)

    def start_gradient(l, c):
        grad_out = gcur[image_rows(c)]
        gg[l, image_rows(c), mine] = grad_out.astype(BF)
        gather_gy(gg, K_G, l, c)

    key_side = masked_lanes(0, 6, -1.0, 640)
    value_side = masked_lanes(6, 6, -1.0, 640)
    row_ids = lax.broadcasted_iota(jnp.int32, (ROWS, 640), 0)
    key_pos = jnp.where(row_ids >= TOK, row_ids - TOK, row_ids) + gx * TOK
    own_ok = key_pos < SEQ
    for c in range(2):
        start_gradient(1, c)

    def backward(step, carry):
        l = 1 - step
        vgrad[V_BD] = row_sum(gcur[...])
        for c in range(2):
            wait_gather(gg, K_G, l, c)
            grad_hid = dot_nt(gg[l, image_rows(c)], by_columns(wdn, l))
            low = (grad_hid * pre[l, image_rows(c)]).astype(BF)
            grad_pre[image_rows(c)] = low
            norm_back_send(
                dot_nt(low, wup[l].reshape(WIDE, 512)), 1, V_MG, K_N2, l, c
            )
        up_sum = row_sum(grad_pre[...].astype(F32))
        for n in range(4):
            vgrad[V_BU + n] = up_sum[:, n * LANES : (n + 1) * LANES]
        store_columns(3, dot_tn(hid[l], gg[l]), l)
        for c in range(2):
            grad_mid = gcur[image_rows(c)] + norm_back_take(1, V_MG, K_N2, l, c, V_MG, V_MS)
            gmid[image_rows(c)] = grad_mid
            gmg[l, image_rows(c), mine] = grad_mid.astype(BF)
            gather_gy(gmg, K_GM, l, c)
        staged[2][l] = dot_tn(norm[1, l], grad_pre[...]).astype(BF).reshape(4, 2, LANES, 512)
        vgrad[V_BO] = row_sum(gmid[...])
        for c in range(2):
            wait_gather(gmg, K_GM, l, c)
            grad_mixed = dot_nt(gmg[l, image_rows(c)], by_columns(wo, l)).astype(BF)
            product = grad_mixed.astype(F32) * attn_f[l, image_rows(c)]
            line = aux[l, image_rows(c)]
            for head in range(2):
                picked = jnp.where(low_half == (head == 0), product, 0.0)
                delta = jnp.sum(picked, axis=-1, keepdims=True)
                for at, piece in enumerate(three_parts(delta)):
                    line = jnp.where(lane_id == 6 + head * 3 + at, piece, line)
            dog[l, c, gx, :, 0:LANES] = grad_mixed
            dog[l, c, gx, :, LANES:] = line.astype(BF)
            for device in gx_peers:
                block = dog.at[l, c, gx]
                put(block, block, do_send.at[l, c], do_recv.at[l, c], device)
        store_columns(1, dot_tn(attn_b[l], gmg[l]), l)
        reduce_start((3, 2, 1), l)

        @pl.when(l == 1)
        def _():
            wait_bytes(qg.at[0, :, 0:7], kv_recv.at[1, 0, 0])
            wait_bytes(qg.at[1, :, 0:7], kv_recv.at[1, 1, 0])

        for c in range(2):
            wait_bytes(dog.at[l, c, 0:7], do_recv.at[l, c])
            all_keys = kv[l, 0, c].reshape(640, LANES)
            all_values = kv[l, 1, c].reshape(640, LANES)
            all_query = qg[l, c].reshape(640, LANES)
            all_grads = dog[l, c].reshape(640, 2 * LANES)
            all_aux = all_grads[:, LANES:]
            all_mixed = all_grads[:, :LANES]
            my_aux = dog[l, c, gx, :, LANES:]
            my_log = jnp.concatenate(
                [my_aux * masked_lanes(0, 3, 1.0, TOK), my_aux * masked_lanes(3, 3, 1.0, TOK)],
                axis=0,
            )
            my_delta = jnp.concatenate(
                [my_aux * masked_lanes(6, 3, 1.0, TOK), my_aux * masked_lanes(9, 3, 1.0, TOK)],
                axis=0,
            )
            my_query = jnp.concatenate([two_heads(qg[l, c, gx]), my_log], axis=1)
            my_mixed = jnp.concatenate([two_heads(dog[l, c, gx, :, 0:LANES]), my_delta], axis=1)
            scores = dot_nt(my_query, jnp.concatenate([all_keys, key_side], axis=1))
            weights = jnp.exp(jnp.where(key_ok, scores, NEG))
            inner = dot_nt(my_mixed, jnp.concatenate([all_values, value_side], axis=1))
            grad_scores = (weights * inner).astype(BF)
            grad_query = join_heads(dot_nn(grad_scores, all_keys)) * 0.125
            owna[image_rows(c), 0:LANES] = grad_query.astype(BF)

            key_log = jnp.concatenate(
                [masked_lanes(0, 3, -1.0, TOK), masked_lanes(3, 3, -1.0, TOK)], axis=0
            )
            key_delta = jnp.concatenate(
                [masked_lanes(6, 3, -1.0, TOK), masked_lanes(9, 3, -1.0, TOK)], axis=0
            )
            my_key = jnp.concatenate([two_heads(kv[l, 0, c, gx]), key_log], axis=1)
            my_value = jnp.concatenate([two_heads(kv[l, 1, c, gx]), key_delta], axis=1)
            scores = dot_nt(my_key, jnp.concatenate([all_query, all_aux], axis=1))
            weights = jnp.exp(jnp.where(own_ok, scores, NEG))
            inner = dot_nt(my_value, all_grads)
            grad_scores = (weights * inner).astype(BF)
            grad_key = join_heads(dot_nn(grad_scores, all_query))
            grad_value = join_heads(dot_nn(weights.astype(BF), all_mixed))
            owna[image_rows(c), LANES : 2 * LANES] = grad_key.astype(BF)
            owna[image_rows(c), 2 * LANES :] = grad_value.astype(BF)
            norm_back_send(
                dot_nt(owna[image_rows(c)], wqkv[l].reshape(WIDE, 384)), 0, V_AG, K_N1, l, c
            )
        staged[0][l] = dot_tn(norm[0, l], owna[...]).astype(BF).reshape(4, 2, LANES, 384)
        reduce_start((0,), l)
        bias_sum = row_sum(owna[...].astype(F32))
        vgrad[V_BQ] = bias_sum[:, :LANES]
        vgrad[V_BV] = bias_sum[:, 2 * LANES :]
        for c in range(2):
            grad_in = gmid[image_rows(c)] + norm_back_take(0, V_AG, K_N1, l, c, V_AG, V_AS)
            igbuf[l, image_rows(c)] = grad_in
            gcur[image_rows(c)] = grad_in.astype(BF).astype(F32)

            @pl.when(l == 1)
            def _(c=c):
                start_gradient(0, c)

        s_vec[l] = vgrad[...]
        send_vec(l)

        @pl.when(l == s)
        def _():
            pltpu.make_async_copy(igbuf.at[l], ig_o.at[s], i_recv.at[0]).start()

        @pl.when(l != s)
        def _():
            put(igbuf.at[l], ig_o.at[s], i_send.at[0], i_recv.at[0], (other, gx, gy))

        reduce_turn((3, 2, 1, 0), l)
        return carry

    lax.fori_loop(0, 2, backward, 0)

    def sum_of(ref):
        total = ref[0].astype(F32)
        for source in range(1, 16):
            total = total + ref[source].astype(F32)
        return total

    def final_sum(group):
        first, second = halves(group)
        wait_bytes(ra2[group].at[0:3], ga2_recv.at[group])
        wait_bytes(rb2[group].at[0:3], gb2_recv.at[group])
        return jnp.concatenate([four(ra2[group]), four(rb2[group])], axis=0)

    g_w_down[...] = final_sum(3)
    g_w_up[...] = final_sum(2)
    g_w_out[...] = final_sum(1)
    total = final_sum(0)
    g_w_query[...] = total[:, :LANES]
    g_w_key[...] = total[:, LANES : 2 * LANES]
    g_w_value[...] = total[:, 2 * LANES :]
    wait_bytes(r_vec.at[0:15], v_recv.at[0])
    total = sum_of(r_vec)
    g_attn_gain[...] = total[V_AG]
    g_attn_shift[...] = total[V_AS]
    g_mlp_gain[...] = total[V_MG]
    g_mlp_shift[...] = total[V_MS]
    g_b_query[...] = total[V_BQ]
    g_b_value[...] = total[V_BV]
    g_b_out[...] = total[V_BO]
    g_b_down[...] = total[V_BD]
    for part in range(4):
        g_b_up[:, part * LANES : (part + 1) * LANES] = total[V_BU + part]
    wait_bytes(act_o, a_recv.at[0])
    wait_bytes(ig_o, i_recv.at[0])

    wait_bytes(ybuf.at[0], a_send.at[0])
    wait_bytes(igbuf.at[0], i_send.at[0])
    wait_bytes(vec.at[s, :, :, 0:896], vec_send.at[0])
    wait_bytes(vec.at[s], vec_send.at[1])
    for group in range(4):
        ref = weights_at[group]
        first, _ = halves(group)
        wait_bytes(ref.at[0, 0:3, 0, first], wa1_send.at[group])
        wait_bytes(ref.at[0, 0:3, 0, first], wb1_send.at[group])
        wait_bytes(ref.at[0, 0:3], wa2_send.at[group])
        wait_bytes(rb2[group].at[0:3], gb2_send.at[group])
        for l in range(2):
            wait_bytes(ref.at[0, 0:3, :, first], wb2_send.at[group, l])
            wait_bytes(ra1[group].at[l, 0:3], ga1_send.at[group, l])
    for l in range(2):
        for c in range(2):
            for kind, buffer in ((K_X, xg), (K_M, mg), (K_G, gg), (K_GM, gmg)):
                wait_bytes(buffer.at[l, image_rows(c), 0:896], gy_send.at[kind, l, c])
            for kind, slot in slot_of.items():
                wait_bytes(rsb.at[slot, l, c, 0:7], gy_send.at[kind, l, c])
            for which in range(2):
                wait_bytes(stat.at[which, l, c, 0:7], st_send.at[which, l, c])
            wait_bytes(kv.at[l, :, c, 0:7], kv_send.at[0, l, c])
            wait_bytes(dog.at[l, c, 0:7], do_send.at[l, c])
        wait_bytes(qg.at[l, :, 0:7], kv_send.at[1, l, 0])
        for count, at in ((1, l), (2, 1 - l)):

            @pl.when(s == at)
            def _(l=l, count=count):
                for group in range(4):
                    wait_bytes(ra2[group].at[0:count], ga2_send.at[group, l])
                    wait_bytes(rb1[group].at[0:count], gb1_send.at[group, l])
                wait_bytes(r_vec.at[0 : 6 + count], v_send.at[l])


def write_out(*refs):
    copies = [
        pltpu.make_async_copy(refs[n], refs[17 + n], refs[34].at[n]) for n in range(17)
    ]
    for copy in copies:
        copy.start()
    for copy in copies:
        copy.wait()


def finish(values):
    return pl.pallas_call(
        write_out,
        out_shape=[jax.ShapeDtypeStruct(value.shape, value.dtype) for value in values],
        in_specs=[pl.BlockSpec(memory_space=pltpu.VMEM)] * 17,
        out_specs=[pl.BlockSpec(memory_space=pl.ANY)] * 17,
        scratch_shapes=[pltpu.SemaphoreType.DMA((17,))],
        name="write_results",
    )(*values)


def local(
    images, counts, attn_gain, attn_shift, w_query, b_query, w_key, w_value, b_value, w_out,
    b_out, mlp_gain, mlp_shift, w_up, b_up, w_down, b_down, cotangent,
):
    anywhere = pl.BlockSpec(memory_space=pl.ANY)
    in_vmem = pl.BlockSpec(memory_space=pltpu.VMEM)
    in_smem = pl.BlockSpec(memory_space=pltpu.SMEM)
    in_specs = [anywhere, in_smem] + [anywhere] * 16
    row = jax.ShapeDtypeStruct((1, LANES), F32)
    square = jax.ShapeDtypeStruct((LANES, LANES), F32)
    out_shape = [
        jax.ShapeDtypeStruct((2, ROWS, LANES), BF),
        jax.ShapeDtypeStruct((2, ROWS, LANES), F32),
        row, row, square, row, square, square, row, square, row, row, row,
        jax.ShapeDtypeStruct((LANES, 512), F32),
        jax.ShapeDtypeStruct((1, 512), F32),
        jax.ShapeDtypeStruct((512, LANES), F32),
        row,
    ]
    vmem = pltpu.VMEM
    scratch = [
        vmem((2, 12, 1, WIDE), F32),
        vmem((ROWS, LANES), BF),
        vmem((2, 4, 2, LANES, 384), BF),
        vmem((2, 4, 2, LANES, LANES), BF),
        vmem((2, 4, 2, LANES, 512), BF),
        vmem((2, 4, 2, 512, LANES), BF),
        vmem((2, ROWS, WIDE), BF),
        vmem((2, ROWS, WIDE), BF),
        vmem((2, ROWS, WIDE), BF),
        vmem((2, ROWS, WIDE), BF),
        vmem((2, 2, ROWS, WIDE), BF),
        vmem((2, 2, ROWS, WIDE), F32),
        vmem((2, 2, ROWS, LANES), F32),
        vmem((ROWS, LANES), F32),
        vmem((ROWS, LANES), F32),
        vmem((ROWS, LANES), F32),
        vmem((ROWS, LANES), F32),
        vmem((4, 2, ROWS, WIDE), BF),
        vmem((4, 2, 2, 8, TOK, LANES), BF),
        vmem((2, 2, 2, 8, 8, LANES), F32),
        vmem((2, 2, 2, 8, TOK, LANES), BF),
        vmem((2, 2, 8, TOK, LANES), BF),
        vmem((2, 2, 8, TOK, 2 * LANES), BF),
        vmem((ROWS, 384), BF),
        vmem((2, ROWS, LANES), F32),
        vmem((2, ROWS, LANES), BF),
        vmem((2, ROWS, LANES), F32),
        vmem((2, ROWS, 512), BF),
        vmem((2, ROWS, 512), F32),
        vmem((ROWS, 512), BF),
        vmem((2, ROWS, LANES), BF),
        vmem((2, ROWS, LANES), F32),
        vmem((2, 12, 1, LANES), F32),
        vmem((16, 12, 1, LANES), F32),
        vmem((12, 1, LANES), F32),
        pltpu.SemaphoreType.DMA((20,)),
        pltpu.SemaphoreType.DMA((8, 2, 2)),
        pltpu.SemaphoreType.DMA((8, 2, 2)),
        pltpu.SemaphoreType.DMA((2, 2, 2)),
        pltpu.SemaphoreType.DMA((2, 2, 2)),
        pltpu.SemaphoreType.DMA((2, 2, 2)),
        pltpu.SemaphoreType.DMA((2, 2, 2)),
        pltpu.SemaphoreType.DMA((2, 2)),
        pltpu.SemaphoreType.DMA((2, 2)),
        pltpu.SemaphoreType.DMA((2,)),
        pltpu.SemaphoreType.DMA((2,)),
        pltpu.SemaphoreType.DMA((4,)),
        pltpu.SemaphoreType.DMA((4,)),
        pltpu.SemaphoreType.DMA((4,)),
        pltpu.SemaphoreType.DMA((4, 2)),
        pltpu.SemaphoreType.DMA((4,)),
        pltpu.SemaphoreType.DMA((4, 2)),
        pltpu.SemaphoreType.DMA((4, 2)),
        pltpu.SemaphoreType.DMA((4, 2)),
        pltpu.SemaphoreType.DMA((4, 2)),
        pltpu.SemaphoreType.DMA((4, 2)),
        pltpu.SemaphoreType.DMA((4, 2)),
        pltpu.SemaphoreType.DMA((4,)),
        pltpu.SemaphoreType.DMA((4, 2)),
        pltpu.SemaphoreType.DMA((4,)),
        pltpu.SemaphoreType.DMA((4,)),
        pltpu.SemaphoreType.DMA((4,)),
        pltpu.SemaphoreType.DMA((2,)),
        pltpu.SemaphoreType.DMA((1,)),
        pltpu.SemaphoreType.DMA((1,)),
        pltpu.SemaphoreType.DMA((1,)),
        pltpu.SemaphoreType.DMA((1,)),
        pltpu.SemaphoreType.DMA((1,)),
    ]
    halved = [(64, 384), (64, LANES), (64, 512), (256, LANES)]
    for lead in (None, (2, 4, 2), (2, 2), (4,), (4, 4), (4,), (4,)):
        for rows, columns in halved:
            if lead is None:
                scratch.append(vmem((2, 4, 2, 2 * rows, columns), BF))
            else:
                scratch.append(vmem(lead + (rows, columns), BF))
    outs = pl.pallas_call(
        kernel,
        out_shape=out_shape,
        in_specs=in_specs,
        out_specs=[in_vmem] * 17,
        scratch_shapes=scratch,
        compiler_params=pltpu.CompilerParams(
            collective_id=0, has_side_effects=True, vmem_limit_bytes=58 * 1024 * 1024
        ),
        cost_estimate=pl.CostEstimate(
            flops=4_000_000_000, bytes_accessed=8_000_000, transcendentals=4_000_000
        ),
        name="two_sections",
    )(
        images.reshape(2, ROWS, LANES), counts, attn_gain, attn_shift, w_query[0], b_query,
        w_key[0], w_value[0], b_value, w_out[0], b_out, mlp_gain, mlp_shift, w_up[0], b_up,
        w_down[0], b_down, cotangent.reshape(2, ROWS, LANES),
    )
    outs = list(finish(outs))
    shape = (1,) + images.shape
    outs[0] = outs[0].reshape(shape)
    outs[1] = outs[1].reshape(shape)
    for index in (4, 6, 7, 9, 13, 15):
        outs[index] = outs[index][None]
    return tuple(outs)


def solution(mesh):
    vector = P("section", "gy")
    in_block = P("section", "gx", "gy")
    out_block = P("section", "gy", "gx")
    rows = P(None, None, "gx", "gy")
    in_specs = (
        rows, P(), vector, vector, in_block, vector, in_block, in_block, vector, out_block,
        vector, vector, vector, in_block, vector, out_block, vector, rows,
    )
    results = P("section", None, None, "gx", "gy")
    out_specs = (
        results, results, vector, vector, in_block, vector, in_block, in_block, vector,
        out_block, vector, vector, vector, in_block, vector, out_block, vector,
    )
    return jax.shard_map(local, mesh=mesh, in_specs=in_specs, out_specs=out_specs, check_vma=False)
```

```python
import jax
import jax.numpy as jnp
from jax import lax
from jax.experimental import pallas as pl
from jax.experimental.pallas import tpu as pltpu
from jax.sharding import PartitionSpec as P

BF = jnp.bfloat16
F32 = jnp.float32
SEQ = 577
EPS = 1e-06
NEG = -1e30
ROWS = 160
TOK = 80
LANES = 128
WIDE = 1024
MESH = pl.DeviceIdType.MESH

K_X, K_O, K_M, K_D, K_G, K_N2, K_GM, K_N1 = range(8)
V_AG, V_AS, V_MG, V_MS, V_BQ, V_BV, V_BO, V_BD, V_BU = range(9)


def dot_nn(a, b):
    return lax.dot_general(a, b, (((1,), (0,)), ((), ())), preferred_element_type=F32)


def dot_nt(a, b):
    return lax.dot_general(a, b, (((1,), (1,)), ((), ())), preferred_element_type=F32)


def dot_tn(a, b):
    return lax.dot_general(a, b, (((0,), (0,)), ((), ())), preferred_element_type=F32)


def lanes(index):
    return pl.ds(pl.multiple_of(index * LANES, LANES), LANES)


def wait_bytes(ref, sem):
    pltpu.make_async_copy(ref, ref, sem).wait()


def put(src, dst, send_sem, recv_sem, device):
    pltpu.make_async_remote_copy(
        src_ref=src,
        dst_ref=dst,
        send_sem=send_sem,
        recv_sem=recv_sem,
        device_id=device,
        device_id_type=MESH,
    ).start()


def image_rows(c):
    return pl.ds(c * TOK, TOK)


def row_sum(values):
    return jnp.sum(values, axis=0, keepdims=True)


def three_parts(values):
    high = values.astype(BF).astype(F32)
    rest = values - high
    mid = rest.astype(BF).astype(F32)
    return high, mid, rest - mid


def kernel(
    images, counts, attn_gain, attn_shift, w_query, b_query, w_key, w_value, b_value, w_out,
    b_out, mlp_gain, mlp_shift, w_up, b_up, w_down, b_down, cotangent,
    act_o, ig_o, g_attn_gain, g_attn_shift, g_w_query, g_b_query, g_w_key, g_w_value, g_b_value,
    g_w_out, g_b_out, g_mlp_gain, g_mlp_shift, g_w_up, g_b_up, g_w_down, g_b_down,
    vec, cot, wqkv, wo, wup, wdn,
    xg, mg, gg, gmg, norm, unit, rstd, res, mid, gcur, gmid,
    stage, rsb, stat, kv, qg, dog, owna, attn_f, attn_b, aux, hid, pre,
    grad_pre, ybuf, igbuf, s_vec, r_vec, vgrad,
    lsem, gy_send, gy_recv, st_send, st_recv, kv_send, kv_recv, do_send, do_recv,
    vec_send, vec_recv, wa1_send, wa1_recv, wa2_send, wa2_recv, wb1_send, wb1_recv, wb2_send,
    wb2_recv, ga1_send, ga1_recv, ga2_send, ga2_recv, gb1_send, gb1_recv, gb2_send, gb2_recv,
    v_send, v_recv, a_send, a_recv, i_send, i_recv, *grad_refs,
):
    staged, ra1, pa, ra2, rb1, pb, rb2 = [grad_refs[4 * n : 4 * n + 4] for n in range(7)]
    weights_at = (wqkv, wo, wup, wdn)
    s = lax.axis_index("section")
    gx = lax.axis_index("gx")
    gy = lax.axis_index("gy")
    other = 1 - s
    mine = lanes(gy)
    x = gx // 2
    h = lax.rem(gx, 2)
    y_slot = h * 2 + s

    barrier = pltpu.get_barrier_semaphore()

    def greet(device):
        pl.semaphore_signal(barrier, inc=1, device_id=device, device_id_type=MESH)

    gy_peers = [(s, gx, lax.rem(gy + k, 8)) for k in (4, 5, 3, 6, 2, 7, 1)]
    far_gx = [(other, lax.rem(gx + k, 8), gy) for k in range(8)]
    far_gy = [(other, gx, lax.rem(gy + k, 8)) for k in range(8)]
    x_peers = [(s, lax.rem(x + k, 4) * 2 + h, gy) for k in (2, 1, 3)]
    gx_peers = [
        (s, lax.rem(x + k, 4) * 2 + side, gy)
        for k, side in ((2, 1 - h), (1, 1 - h), (3, 1 - h), (2, h), (0, 1 - h), (1, h), (3, h))
    ]
    y_peers = [(s, x * 2 + 1 - h, gy), (other, gx, gy), (other, x * 2 + 1 - h, gy)]
    for device in gy_peers + gx_peers + far_gx + far_gy[1:]:
        greet(device)

    own = [pltpu.make_async_copy(images.at[s], xg.at[0, :, mine], lsem.at[0])]
    own.append(pltpu.make_async_copy(cotangent.at[s], cot, lsem.at[1]))
    rows = [attn_gain, attn_shift, mlp_gain, mlp_shift, b_query, b_value, b_out, b_down]
    vec_own = []
    for row, ref in enumerate(rows):
        vec_own.append(pltpu.make_async_copy(ref, vec.at[s, row, :, mine], lsem.at[8 + row]))
    for part in range(4):
        vec_own.append(
            pltpu.make_async_copy(
                b_up.at[:, part * LANES : (part + 1) * LANES],
                vec.at[s, V_BU + part, :, mine],
                lsem.at[16 + part],
            )
        )
    w_own = []
    for part, ref in enumerate((w_query, w_key, w_value)):
        w_own.append(
            pltpu.make_async_copy(
                ref, wqkv.at[s, x, h, :, part * LANES : (part + 1) * LANES], lsem.at[2 + part]
            )
        )
    w_own.append(pltpu.make_async_copy(w_out, wo.at[s, x, h], lsem.at[5]))
    w_own.append(pltpu.make_async_copy(w_up, wup.at[s, x, h], lsem.at[6]))
    w_own.append(pltpu.make_async_copy(w_down, wdn.at[s, x, h], lsem.at[7]))
    for copy in own + vec_own + w_own:
        copy.start()

    pl.semaphore_wait(barrier, 29)

    for c in range(2):
        for device in gy_peers:
            put(
                images.at[s, image_rows(c)],
                xg.at[0, image_rows(c), mine],
                gy_send.at[K_X, 0, c],
                gy_recv.at[K_X, 0, c],
                device,
            )
    for copy in vec_own:
        copy.wait()
    for near, group in ((0, gy_peers), (1, far_gy)):
        for device in group:
            block = vec.at[s, :, :, mine]
            put(block, block, vec_send.at[near], vec_recv.at[near], device)
    for copy in w_own:
        copy.wait()
    own[0].wait()
    own[1].wait()

    half_rows = (64, 64, 64, 256)

    def halves(group):
        return pl.ds(0, half_rows[group]), pl.ds(half_rows[group], half_rows[group])

    def spread_own(groups):
        for group in groups:
            ref = weights_at[group]
            first, second = halves(group)
            block = ref.at[s, x, h, first]
            for device in x_peers:
                put(block, block, wa1_send.at[group], wa1_recv.at[group], device)
            block = ref.at[s, x, h, second]
            for device in y_peers:
                put(block, block, wb1_send.at[group], wb1_recv.at[group, s], device)

    def pass_on(groups, l):
        for group in groups:
            ref = weights_at[group]
            first, second = halves(group)

            @pl.when(l == s)
            def _(ref=ref, first=first, group=group):
                wait_bytes(ref.at[l, 0:3, 0, first], wa1_recv.at[group])
                block = ref.at[s, :, h, first]
                for device in y_peers:
                    put(block, block, wa2_send.at[group], wa2_recv.at[group, s], device)
                wait_bytes(ref.at[l, 0, 0, first], wb1_recv.at[group, l])

            @pl.when(l != s)
            def _(ref=ref, first=first, group=group):
                wait_bytes(ref.at[l, 0, :, first], wb1_recv.at[group, l])

            block = ref.at[l, x, :, second]
            for device in x_peers:
                put(block, block, wb2_send.at[group, l], wb2_recv.at[group, l], device)

    def wait_weights(group, l):
        ref = weights_at[group]
        first, _ = halves(group)

        @pl.when(l == s)
        def _():
            wait_bytes(ref.at[l, :, 0, first], wa2_recv.at[group, l])

        @pl.when(l != s)
        def _():
            wait_bytes(ref.at[l, :, :, first], wa2_recv.at[group, l])

        wait_bytes(ref.at[l, 0:3, :, first], wb2_recv.at[group, l])

    def by_columns(ref, l):
        return jnp.concatenate([ref[l, a, b] for a in range(4) for b in range(2)], axis=1)

    spread_own((0, 1, 2, 3))

    def gather_gy(buffer, kind, l, c):
        block = buffer.at[l, image_rows(c), mine]
        for device in gy_peers:
            put(block, block, gy_send.at[kind, l, c], gy_recv.at[kind, l, c], device)

    def wait_gather(buffer, kind, l, c):
        wait_bytes(buffer.at[l, image_rows(c), 0:896], gy_recv.at[kind, l, c])

    slot_of = {K_O: 0, K_D: 1, K_N2: 2, K_N1: 3}

    def scatter_gy(partial, kind, l, c):
        slot = slot_of[kind]
        stage[slot, l, image_rows(c)] = partial.astype(BF)
        for _, _, peer in gy_peers:
            put(
                stage.at[slot, l, image_rows(c), lanes(peer)],
                rsb.at[slot, l, c, gy],
                gy_send.at[kind, l, c],
                gy_recv.at[kind, l, c],
                (s, gx, peer),
            )
        rsb[slot, l, c, gy] = stage[slot, l, image_rows(c), mine]

    def wait_scatter(kind, l, c):
        slot = slot_of[kind]
        wait_bytes(rsb.at[slot, l, c, 0:7], gy_recv.at[kind, l, c])
        total = rsb[slot, l, c, 0].astype(F32)
        for source in range(1, 8):
            total = total + rsb[slot, l, c, source].astype(F32)
        return total

    lane_id = lax.broadcasted_iota(jnp.int32, (TOK, LANES), 1)
    low_half = lane_id < 64
    head_mask = [low_half.astype(F32).astype(BF), (lane_id >= 64).astype(F32).astype(BF)]

    def two_heads(block):
        return jnp.concatenate([block * head_mask[0], block * head_mask[1]], axis=0)

    def join_heads(both):
        return jnp.where(low_half, both[:TOK], both[TOK:])

    def masked_lanes(low, count, value, height):
        ids = lax.broadcasted_iota(jnp.int32, (height, LANES), 1)
        return jnp.where((ids >= low) & (ids < low + count), value, 0.0).astype(BF)

    key_ok = lax.broadcasted_iota(jnp.int32, (ROWS, 640), 1) < SEQ

    def norm_rows(values, gain_row, shift_row, which, l, c):
        center = values - jnp.mean(values, axis=-1, keepdims=True)
        spread = jnp.mean(center * center, axis=-1, keepdims=True)
        scale = lax.rsqrt(spread + EPS)
        xhat = center * scale
        unit[which, l, image_rows(c)] = xhat
        rstd[which, l, image_rows(c)] = jnp.broadcast_to(scale, (TOK, LANES))
        normed = (xhat * vec[l, gain_row] + vec[l, shift_row]).astype(BF)
        norm[which, l, image_rows(c)] = normed
        return normed

    row_id = lax.broadcasted_iota(jnp.int32, (ROWS, LANES), 0)
    image_id = (row_id >= TOK).astype(jnp.int32)
    position = row_id - image_id * TOK + gx * TOK
    live = ((image_id < counts[s]) & (position < SEQ)).astype(F32)
    gcur[...] = cot[...].astype(F32) * live

    def start_gradient(l, c):
        grad_out = gcur[image_rows(c)]
        gg[l, image_rows(c), mine] = grad_out.astype(BF)
        gather_gy(gg, K_G, l, c)

    res[...] = xg[0, :, mine].astype(F32)
    wait_bytes(vec.at[s, :, :, 0:896], vec_recv.at[0])
    wait_bytes(vec.at[other], vec_recv.at[1])

    def finish_layer(l):
        for c in range(2):
            output = mid[image_rows(c)] + wait_scatter(K_D, l, c) + vec[l, V_BD, :, mine]
            output = output.astype(BF)
            ybuf[l, image_rows(c)] = output
            if l == 0:
                res[image_rows(c)] = output.astype(F32)
                xg[1, image_rows(c), mine] = output
                gather_gy(xg, K_X, 1, c)

        @pl.when(s == l)
        def _():
            pltpu.make_async_copy(ybuf.at[l], act_o.at[s], a_recv.at[0]).start()

        @pl.when(s != l)
        def _():
            put(ybuf.at[l], act_o.at[s], a_send.at[0], a_recv.at[0], (other, gx, gy))

    def forward(l, carry):
        for c in range(2):
            wait_gather(xg, K_X, l, c)
            normed = norm_rows(xg[l, image_rows(c)].astype(F32), V_AG, V_AS, 0, l, c)
            if c == 0:

                @pl.when(l == 0)
                def _():
                    pass_on((0,), 0)

                wait_weights(0, l)
            qkv = dot_nn(normed, wqkv[l].reshape(WIDE, 384))
            kv[l, 0, c, gx] = qkv[:, LANES : 2 * LANES].astype(BF)
            kv[l, 1, c, gx] = (qkv[:, 2 * LANES :] + vec[l, V_BV, :, mine]).astype(BF)
            query = (qkv[:, :LANES] + vec[l, V_BQ, :, mine]).astype(BF)
            qg[l, c, gx] = query * jnp.asarray(0.125, BF)
            for device in gx_peers:
                block = kv.at[l, :, c, gx]
                put(block, block, kv_send.at[0, l, c], kv_recv.at[0, l, c], device)
        for device in gx_peers:
            block = qg.at[l, :, gx]
            put(block, block, kv_send.at[1, l, 0], kv_recv.at[1, l, 0], device)

        @pl.when(l == 0)
        def _():
            pass_on((1, 2, 3), 0)

        @pl.when(l == 1)
        def _():
            for c in range(2):
                start_gradient(1, c)

        for c in range(2):
            wait_bytes(kv.at[l, :, c, 0:7], kv_recv.at[0, l, c])
            all_keys = kv[l, 0, c].reshape(640, LANES)
            all_values = kv[l, 1, c].reshape(640, LANES)
            scores = dot_nt(two_heads(qg[l, c, gx]), all_keys)
            scores = jnp.where(key_ok, scores, NEG)
            highest = jnp.max(scores, axis=-1, keepdims=True)
            exponent = jnp.exp(scores - highest)
            summed = jnp.sum(exponent, axis=-1, keepdims=True)
            full = exponent / summed
            weights = full.astype(BF)
            mixed = join_heads(dot_nn(weights, all_values))
            mixed_low = mixed.astype(BF)
            attn_b[l, image_rows(c)] = mixed_low
            if c == 0:
                wait_weights(1, l)
            scatter_gy(dot_nn(mixed_low, by_columns(wo, l)), K_O, l, c)
            left_out = (full - weights.astype(F32)).astype(BF)
            attn_f[l, image_rows(c)] = mixed + join_heads(dot_nn(left_out, all_values))
            logs = highest + jnp.log(summed)
            line = jnp.zeros((TOK, LANES), F32)
            for head in range(2):
                for at, piece in enumerate(three_parts(logs[head * TOK : (head + 1) * TOK])):
                    line = jnp.where(lane_id == head * 3 + at, piece, line)
            aux[l, image_rows(c)] = line

        @pl.when(l == 0)
        def _():
            pass_on((0, 1), 1)

        for c in range(2):
            middle = res[image_rows(c)] + wait_scatter(K_O, l, c) + vec[l, V_BO, :, mine]
            mid[image_rows(c)] = middle
            mg[l, image_rows(c), mine] = middle.astype(BF)
            gather_gy(mg, K_M, l, c)

        @pl.when(l == 0)
        def _():
            pass_on((2, 3), 1)

        bias = jnp.concatenate([vec[l, V_BU + n, :, mine] for n in range(4)], axis=1)
        for c in range(2):
            wait_gather(mg, K_M, l, c)
            normed = norm_rows(mg[l, image_rows(c)].astype(F32), V_MG, V_MS, 1, l, c)
            if c == 0:
                wait_weights(2, l)
            pre_act = dot_nn(normed, wup[l].reshape(WIDE, 512)) + bias
            gate = 0.5 * (1.0 + lax.erf(pre_act * 0.7071067811865476))
            hidden = (pre_act * gate).astype(BF)
            hid[l, image_rows(c)] = hidden
            if c == 0:
                wait_weights(3, l)
            scatter_gy(dot_nn(hidden, by_columns(wdn, l)), K_D, l, c)
            slope = jnp.exp(-0.5 * pre_act * pre_act) * 0.3989422804014327
            pre[l, image_rows(c)] = gate + pre_act * slope

        @pl.when(l == 0)
        def _():
            finish_layer(0)

        return carry

    lax.fori_loop(0, 2, forward, 0)

    def reduce_start(groups, l):
        for group in groups:
            first, second = halves(group)
            ref = staged[group]
            for _, peer, _ in x_peers:
                put(
                    ref.at[l, peer // 2, :, first],
                    ra1[group].at[l, x],
                    ga1_send.at[group, l],
                    ga1_recv.at[group, l],
                    (s, peer, gy),
                )
            put(
                ref.at[l, :, 1 - h, second],
                rb1[group].at[y_slot],
                gb1_send.at[group, l],
                gb1_recv.at[group],
                (l, x * 2 + 1 - h, gy),
            )

            @pl.when(l != s)
            def _(ref=ref, second=second, group=group):
                put(
                    ref.at[l, :, h, second],
                    rb1[group].at[y_slot],
                    gb1_send.at[group, l],
                    gb1_recv.at[group],
                    (l, gx, gy),
                )

            ra1[group][l, x] = ref[l, x, :, first]

            @pl.when(l == s)
            def _(ref=ref, second=second, group=group):
                rb1[group][y_slot] = ref[l, :, h, second]

    def four(ref, index=None):
        parts = [(ref[n] if index is None else ref[index, n]).astype(F32) for n in range(4)]
        return (parts[0] + parts[1]) + (parts[2] + parts[3])

    def reduce_turn(groups, l):
        for group in groups:
            wait_bytes(ra1[group].at[l, 0:3], ga1_recv.at[group, l])
            pa[group][l] = four(ra1[group], l).astype(BF)
            put(
                pa[group].at[l, 1 - h],
                ra2[group].at[y_slot],
                ga2_send.at[group, l],
                ga2_recv.at[group],
                (l, x * 2 + 1 - h, gy),
            )

            @pl.when(l != s)
            def _(group=group):
                put(
                    pa[group].at[l, h],
                    ra2[group].at[y_slot],
                    ga2_send.at[group, l],
                    ga2_recv.at[group],
                    (l, gx, gy),
                )

            @pl.when(l == s)
            def _(group=group):
                ra2[group][y_slot] = pa[group][l, h]
                wait_bytes(rb1[group].at[0:3], gb1_recv.at[group])
                pb[group][...] = four(rb1[group]).astype(BF)
                for _, peer, _ in x_peers:
                    put(
                        pb[group].at[peer // 2],
                        rb2[group].at[x],
                        gb2_send.at[group],
                        gb2_recv.at[group],
                        (s, peer, gy),
                    )
                rb2[group][x] = pb[group][x]

    def send_vec(l):
        for j in range(8):
            k = lax.rem(gx + j, 8)
            dst = r_vec.at[s * 8 + gx]
            if j == 0:

                @pl.when(l == s)
                def _():
                    r_vec[s * 8 + gx] = s_vec[l]

                @pl.when(l != s)
                def _(k=k):
                    put(s_vec.at[l], r_vec.at[s * 8 + gx], v_send.at[l], v_recv.at[0], (l, k, gy))

            else:
                put(s_vec.at[l], dst, v_send.at[l], v_recv.at[0], (l, k, gy))

    def send_stats(first, second, which, l, c):
        ids = lax.broadcasted_iota(jnp.int32, (TOK, LANES), 1)
        both = jnp.where(ids == 0, first, jnp.where(ids == 1, second, 0.0))
        both = jnp.concatenate([both, jnp.zeros((LANES - TOK, LANES), F32)], axis=0)
        stat[which, l, c, gy] = both.T[:8]
        for device in gy_peers:
            block = stat.at[which, l, c, gy]
            put(block, block, st_send.at[which, l, c], st_recv.at[which, l, c], device)

    def wait_stats(which, l, c):
        wait_bytes(stat.at[which, l, c, 0:7], st_recv.at[which, l, c])
        total = stat[which, l, c, 0]
        for source in range(1, 8):
            total = total + stat[which, l, c, source]
        total = jnp.concatenate([total, jnp.zeros((LANES - 8, LANES), F32)], axis=0).T
        return total[:TOK, 0:1], total[:TOK, 1:2]

    def norm_back_send(partial, which, gain_row, kind, l, c):
        scatter_gy(partial, kind, l, c)
        weighted = partial * vec[l, gain_row]
        first = jnp.sum(weighted, axis=-1, keepdims=True)
        second = jnp.sum(weighted * unit[which, l, image_rows(c)], axis=-1, keepdims=True)
        send_stats(first, second, which, l, c)

    def add_vec(slot, value, c):
        if c == 0:
            vgrad[slot] = value
        else:
            vgrad[slot] += value

    def norm_back_take(which, gain_row, kind, l, c, gain_slot, shift_slot):
        grad = wait_scatter(kind, l, c)
        first, second = wait_stats(which, l, c)
        xhat = unit[which, l, image_rows(c), mine]
        add_vec(gain_slot, row_sum(grad * xhat), c)
        add_vec(shift_slot, row_sum(grad), c)
        inner = grad * vec[l, gain_row, :, mine]
        return rstd[which, l, image_rows(c)] * (
            inner - first * (1.0 / WIDE) - xhat * (second * (1.0 / WIDE))
        )

    def store_columns(group, grad, l):
        for block in range(8):
            columns = grad[:, block * LANES : (block + 1) * LANES]
            staged[group][l, block // 2, block % 2] = columns.astype(BF)

    key_side = masked_lanes(0, 6, -1.0, 640)
    value_side = masked_lanes(6, 6, -1.0, 640)
    row_ids = lax.broadcasted_iota(jnp.int32, (ROWS, 640), 0)
    key_pos = jnp.where(row_ids >= TOK, row_ids - TOK, row_ids) + gx * TOK
    own_ok = key_pos < SEQ
    def backward(step, carry):
        l = 1 - step
        vgrad[V_BD] = row_sum(gcur[...])
        for c in range(2):
            wait_gather(gg, K_G, l, c)
            grad_hid = dot_nt(gg[l, image_rows(c)], by_columns(wdn, l))
            low = (grad_hid * pre[l, image_rows(c)]).astype(BF)
            grad_pre[image_rows(c)] = low
            norm_back_send(
                dot_nt(low, wup[l].reshape(WIDE, 512)), 1, V_MG, K_N2, l, c
            )
        up_sum = row_sum(grad_pre[...].astype(F32))
        for n in range(4):
            vgrad[V_BU + n] = up_sum[:, n * LANES : (n + 1) * LANES]
        store_columns(3, dot_tn(hid[l], gg[l]), l)
        reduce_start((3,), l)

        @pl.when(l == 0)
        def _():
            reduce_turn((0,), 1)

        @pl.when(l == 1)
        def _():
            finish_layer(1)

        for c in range(2):
            grad_mid = gcur[image_rows(c)] + norm_back_take(1, V_MG, K_N2, l, c, V_MG, V_MS)
            gmid[image_rows(c)] = grad_mid
            gmg[l, image_rows(c), mine] = grad_mid.astype(BF)
            gather_gy(gmg, K_GM, l, c)
        staged[2][l] = dot_tn(norm[1, l], grad_pre[...]).astype(BF).reshape(4, 2, LANES, 512)
        reduce_start((2,), l)
        vgrad[V_BO] = row_sum(gmid[...])
        for c in range(2):
            wait_gather(gmg, K_GM, l, c)
            grad_mixed = dot_nt(gmg[l, image_rows(c)], by_columns(wo, l)).astype(BF)
            product = grad_mixed.astype(F32) * attn_f[l, image_rows(c)]
            line = aux[l, image_rows(c)]
            for head in range(2):
                picked = jnp.where(low_half == (head == 0), product, 0.0)
                delta = jnp.sum(picked, axis=-1, keepdims=True)
                for at, piece in enumerate(three_parts(delta)):
                    line = jnp.where(lane_id == 6 + head * 3 + at, piece, line)
            dog[l, c, gx, :, 0:LANES] = grad_mixed
            dog[l, c, gx, :, LANES:] = line.astype(BF)
            for device in gx_peers:
                block = dog.at[l, c, gx]
                put(block, block, do_send.at[l, c], do_recv.at[l, c], device)
        store_columns(1, dot_tn(attn_b[l], gmg[l]), l)
        reduce_start((1,), l)
        reduce_turn((3,), l)

        @pl.when(l == 1)
        def _():
            wait_bytes(qg.at[0, :, 0:7], kv_recv.at[1, 0, 0])
            wait_bytes(qg.at[1, :, 0:7], kv_recv.at[1, 1, 0])

        for c in range(2):
            wait_bytes(dog.at[l, c, 0:7], do_recv.at[l, c])
            all_keys = kv[l, 0, c].reshape(640, LANES)
            all_values = kv[l, 1, c].reshape(640, LANES)
            all_query = qg[l, c].reshape(640, LANES)
            all_grads = dog[l, c].reshape(640, 2 * LANES)
            all_aux = all_grads[:, LANES:]
            all_mixed = all_grads[:, :LANES]
            my_aux = dog[l, c, gx, :, LANES:]
            my_log = jnp.concatenate(
                [my_aux * masked_lanes(0, 3, 1.0, TOK), my_aux * masked_lanes(3, 3, 1.0, TOK)],
                axis=0,
            )
            my_delta = jnp.concatenate(
                [my_aux * masked_lanes(6, 3, 1.0, TOK), my_aux * masked_lanes(9, 3, 1.0, TOK)],
                axis=0,
            )
            my_query = jnp.concatenate([two_heads(qg[l, c, gx]), my_log], axis=1)
            my_mixed = jnp.concatenate([two_heads(dog[l, c, gx, :, 0:LANES]), my_delta], axis=1)
            scores = dot_nt(my_query, jnp.concatenate([all_keys, key_side], axis=1))
            weights = jnp.exp(jnp.where(key_ok, scores, NEG))
            inner = dot_nt(my_mixed, jnp.concatenate([all_values, value_side], axis=1))
            grad_scores = (weights * inner).astype(BF)
            grad_query = join_heads(dot_nn(grad_scores, all_keys)) * 0.125
            owna[image_rows(c), 0:LANES] = grad_query.astype(BF)

            key_log = jnp.concatenate(
                [masked_lanes(0, 3, -1.0, TOK), masked_lanes(3, 3, -1.0, TOK)], axis=0
            )
            key_delta = jnp.concatenate(
                [masked_lanes(6, 3, -1.0, TOK), masked_lanes(9, 3, -1.0, TOK)], axis=0
            )
            my_key = jnp.concatenate([two_heads(kv[l, 0, c, gx]), key_log], axis=1)
            my_value = jnp.concatenate([two_heads(kv[l, 1, c, gx]), key_delta], axis=1)
            scores = dot_nt(my_key, jnp.concatenate([all_query, all_aux], axis=1))
            weights = jnp.exp(jnp.where(own_ok, scores, NEG))
            inner = dot_nt(my_value, all_grads)
            grad_scores = (weights * inner).astype(BF)
            grad_key = join_heads(dot_nn(grad_scores, all_query))
            grad_value = join_heads(dot_nn(weights.astype(BF), all_mixed))
            owna[image_rows(c), LANES : 2 * LANES] = grad_key.astype(BF)
            owna[image_rows(c), 2 * LANES :] = grad_value.astype(BF)
            norm_back_send(
                dot_nt(owna[image_rows(c)], wqkv[l].reshape(WIDE, 384)), 0, V_AG, K_N1, l, c
            )
        staged[0][l] = dot_tn(norm[0, l], owna[...]).astype(BF).reshape(4, 2, LANES, 384)
        reduce_start((0,), l)
        reduce_turn((2, 1), l)
        bias_sum = row_sum(owna[...].astype(F32))
        vgrad[V_BQ] = bias_sum[:, :LANES]
        vgrad[V_BV] = bias_sum[:, 2 * LANES :]
        for c in range(2):
            grad_in = gmid[image_rows(c)] + norm_back_take(0, V_AG, K_N1, l, c, V_AG, V_AS)
            igbuf[l, image_rows(c)] = grad_in
            gcur[image_rows(c)] = grad_in.astype(BF).astype(F32)

            @pl.when(l == 1)
            def _(c=c):
                start_gradient(0, c)

        s_vec[l] = vgrad[...]
        send_vec(l)

        @pl.when(l == s)
        def _():
            pltpu.make_async_copy(igbuf.at[l], ig_o.at[s], i_recv.at[0]).start()

        @pl.when(l != s)
        def _():
            put(igbuf.at[l], ig_o.at[s], i_send.at[0], i_recv.at[0], (other, gx, gy))

        @pl.when(l == 0)
        def _():
            reduce_turn((0,), 0)

        return carry

    lax.fori_loop(0, 2, backward, 0)

    def sum_of(ref):
        total = ref[0].astype(F32)
        for source in range(1, 16):
            total = total + ref[source].astype(F32)
        return total

    def final_sum(group):
        first, second = halves(group)
        wait_bytes(ra2[group].at[0:3], ga2_recv.at[group])
        wait_bytes(rb2[group].at[0:3], gb2_recv.at[group])
        return jnp.concatenate([four(ra2[group]), four(rb2[group])], axis=0)

    g_w_down[...] = final_sum(3)
    g_w_up[...] = final_sum(2)
    g_w_out[...] = final_sum(1)
    total = final_sum(0)
    g_w_query[...] = total[:, :LANES]
    g_w_key[...] = total[:, LANES : 2 * LANES]
    g_w_value[...] = total[:, 2 * LANES :]
    wait_bytes(r_vec.at[0:15], v_recv.at[0])
    total = sum_of(r_vec)
    g_attn_gain[...] = total[V_AG]
    g_attn_shift[...] = total[V_AS]
    g_mlp_gain[...] = total[V_MG]
    g_mlp_shift[...] = total[V_MS]
    g_b_query[...] = total[V_BQ]
    g_b_value[...] = total[V_BV]
    g_b_out[...] = total[V_BO]
    g_b_down[...] = total[V_BD]
    for part in range(4):
        g_b_up[:, part * LANES : (part + 1) * LANES] = total[V_BU + part]
    wait_bytes(act_o, a_recv.at[0])
    wait_bytes(ig_o, i_recv.at[0])

    wait_bytes(ybuf.at[0], a_send.at[0])
    wait_bytes(igbuf.at[0], i_send.at[0])
    wait_bytes(vec.at[s, :, :, 0:896], vec_send.at[0])
    wait_bytes(vec.at[s], vec_send.at[1])
    for group in range(4):
        ref = weights_at[group]
        first, _ = halves(group)
        wait_bytes(ref.at[0, 0:3, 0, first], wa1_send.at[group])
        wait_bytes(ref.at[0, 0:3, 0, first], wb1_send.at[group])
        wait_bytes(ref.at[0, 0:3], wa2_send.at[group])
        wait_bytes(rb2[group].at[0:3], gb2_send.at[group])
        for l in range(2):
            wait_bytes(ref.at[0, 0:3, :, first], wb2_send.at[group, l])
            wait_bytes(ra1[group].at[l, 0:3], ga1_send.at[group, l])
    for l in range(2):
        for c in range(2):
            for kind, buffer in ((K_X, xg), (K_M, mg), (K_G, gg), (K_GM, gmg)):
                wait_bytes(buffer.at[l, image_rows(c), 0:896], gy_send.at[kind, l, c])
            for kind, slot in slot_of.items():
                wait_bytes(rsb.at[slot, l, c, 0:7], gy_send.at[kind, l, c])
            for which in range(2):
                wait_bytes(stat.at[which, l, c, 0:7], st_send.at[which, l, c])
            wait_bytes(kv.at[l, :, c, 0:7], kv_send.at[0, l, c])
            wait_bytes(dog.at[l, c, 0:7], do_send.at[l, c])
        wait_bytes(qg.at[l, :, 0:7], kv_send.at[1, l, 0])
        for count, at in ((1, l), (2, 1 - l)):

            @pl.when(s == at)
            def _(l=l, count=count):
                for group in range(4):
                    wait_bytes(ra2[group].at[0:count], ga2_send.at[group, l])
                    wait_bytes(rb1[group].at[0:count], gb1_send.at[group, l])
                wait_bytes(r_vec.at[0 : 6 + count], v_send.at[l])


def write_out(*refs):
    copies = [
        pltpu.make_async_copy(refs[n], refs[17 + n], refs[34].at[n]) for n in range(17)
    ]
    for copy in copies:
        copy.start()
    for copy in copies:
        copy.wait()


def finish(values):
    return pl.pallas_call(
        write_out,
        out_shape=[jax.ShapeDtypeStruct(value.shape, value.dtype) for value in values],
        in_specs=[pl.BlockSpec(memory_space=pltpu.VMEM)] * 17,
        out_specs=[pl.BlockSpec(memory_space=pl.ANY)] * 17,
        scratch_shapes=[pltpu.SemaphoreType.DMA((17,))],
        name="write_results",
    )(*values)


def local(
    images, counts, attn_gain, attn_shift, w_query, b_query, w_key, w_value, b_value, w_out,
    b_out, mlp_gain, mlp_shift, w_up, b_up, w_down, b_down, cotangent,
):
    anywhere = pl.BlockSpec(memory_space=pl.ANY)
    in_vmem = pl.BlockSpec(memory_space=pltpu.VMEM)
    in_smem = pl.BlockSpec(memory_space=pltpu.SMEM)
    in_specs = [anywhere, in_smem] + [anywhere] * 16
    row = jax.ShapeDtypeStruct((1, LANES), F32)
    square = jax.ShapeDtypeStruct((LANES, LANES), F32)
    out_shape = [
        jax.ShapeDtypeStruct((2, ROWS, LANES), BF),
        jax.ShapeDtypeStruct((2, ROWS, LANES), F32),
        row, row, square, row, square, square, row, square, row, row, row,
        jax.ShapeDtypeStruct((LANES, 512), F32),
        jax.ShapeDtypeStruct((1, 512), F32),
        jax.ShapeDtypeStruct((512, LANES), F32),
        row,
    ]
    vmem = pltpu.VMEM
    scratch = [
        vmem((2, 12, 1, WIDE), F32),
        vmem((ROWS, LANES), BF),
        vmem((2, 4, 2, LANES, 384), BF),
        vmem((2, 4, 2, LANES, LANES), BF),
        vmem((2, 4, 2, LANES, 512), BF),
        vmem((2, 4, 2, 512, LANES), BF),
        vmem((2, ROWS, WIDE), BF),
        vmem((2, ROWS, WIDE), BF),
        vmem((2, ROWS, WIDE), BF),
        vmem((2, ROWS, WIDE), BF),
        vmem((2, 2, ROWS, WIDE), BF),
        vmem((2, 2, ROWS, WIDE), F32),
        vmem((2, 2, ROWS, LANES), F32),
        vmem((ROWS, LANES), F32),
        vmem((ROWS, LANES), F32),
        vmem((ROWS, LANES), F32),
        vmem((ROWS, LANES), F32),
        vmem((4, 2, ROWS, WIDE), BF),
        vmem((4, 2, 2, 8, TOK, LANES), BF),
        vmem((2, 2, 2, 8, 8, LANES), F32),
        vmem((2, 2, 2, 8, TOK, LANES), BF),
        vmem((2, 2, 8, TOK, LANES), BF),
        vmem((2, 2, 8, TOK, 2 * LANES), BF),
        vmem((ROWS, 384), BF),
        vmem((2, ROWS, LANES), F32),
        vmem((2, ROWS, LANES), BF),
        vmem((2, ROWS, LANES), F32),
        vmem((2, ROWS, 512), BF),
        vmem((2, ROWS, 512), F32),
        vmem((ROWS, 512), BF),
        vmem((2, ROWS, LANES), BF),
        vmem((2, ROWS, LANES), F32),
        vmem((2, 12, 1, LANES), F32),
        vmem((16, 12, 1, LANES), F32),
        vmem((12, 1, LANES), F32),
        pltpu.SemaphoreType.DMA((20,)),
        pltpu.SemaphoreType.DMA((8, 2, 2)),
        pltpu.SemaphoreType.DMA((8, 2, 2)),
        pltpu.SemaphoreType.DMA((2, 2, 2)),
        pltpu.SemaphoreType.DMA((2, 2, 2)),
        pltpu.SemaphoreType.DMA((2, 2, 2)),
        pltpu.SemaphoreType.DMA((2, 2, 2)),
        pltpu.SemaphoreType.DMA((2, 2)),
        pltpu.SemaphoreType.DMA((2, 2)),
        pltpu.SemaphoreType.DMA((2,)),
        pltpu.SemaphoreType.DMA((2,)),
        pltpu.SemaphoreType.DMA((4,)),
        pltpu.SemaphoreType.DMA((4,)),
        pltpu.SemaphoreType.DMA((4,)),
        pltpu.SemaphoreType.DMA((4, 2)),
        pltpu.SemaphoreType.DMA((4,)),
        pltpu.SemaphoreType.DMA((4, 2)),
        pltpu.SemaphoreType.DMA((4, 2)),
        pltpu.SemaphoreType.DMA((4, 2)),
        pltpu.SemaphoreType.DMA((4, 2)),
        pltpu.SemaphoreType.DMA((4, 2)),
        pltpu.SemaphoreType.DMA((4, 2)),
        pltpu.SemaphoreType.DMA((4,)),
        pltpu.SemaphoreType.DMA((4, 2)),
        pltpu.SemaphoreType.DMA((4,)),
        pltpu.SemaphoreType.DMA((4,)),
        pltpu.SemaphoreType.DMA((4,)),
        pltpu.SemaphoreType.DMA((2,)),
        pltpu.SemaphoreType.DMA((1,)),
        pltpu.SemaphoreType.DMA((1,)),
        pltpu.SemaphoreType.DMA((1,)),
        pltpu.SemaphoreType.DMA((1,)),
        pltpu.SemaphoreType.DMA((1,)),
    ]
    halved = [(64, 384), (64, LANES), (64, 512), (256, LANES)]
    for lead in (None, (2, 4, 2), (2, 2), (4,), (4, 4), (4,), (4,)):
        for rows, columns in halved:
            if lead is None:
                scratch.append(vmem((2, 4, 2, 2 * rows, columns), BF))
            else:
                scratch.append(vmem(lead + (rows, columns), BF))
    outs = pl.pallas_call(
        kernel,
        out_shape=out_shape,
        in_specs=in_specs,
        out_specs=[in_vmem] * 17,
        scratch_shapes=scratch,
        compiler_params=pltpu.CompilerParams(
            collective_id=0, has_side_effects=True, vmem_limit_bytes=58 * 1024 * 1024
        ),
        cost_estimate=pl.CostEstimate(
            flops=4_000_000_000, bytes_accessed=8_000_000, transcendentals=4_000_000
        ),
        name="two_sections",
    )(
        images.reshape(2, ROWS, LANES), counts, attn_gain, attn_shift, w_query[0], b_query,
        w_key[0], w_value[0], b_value, w_out[0], b_out, mlp_gain, mlp_shift, w_up[0], b_up,
        w_down[0], b_down, cotangent.reshape(2, ROWS, LANES),
    )
    outs = list(finish(outs))
    shape = (1,) + images.shape
    outs[0] = outs[0].reshape(shape)
    outs[1] = outs[1].reshape(shape)
    for index in (4, 6, 7, 9, 13, 15):
        outs[index] = outs[index][None]
    return tuple(outs)


def solution(mesh):
    vector = P("section", "gy")
    in_block = P("section", "gx", "gy")
    out_block = P("section", "gy", "gx")
    rows = P(None, None, "gx", "gy")
    in_specs = (
        rows, P(), vector, vector, in_block, vector, in_block, in_block, vector, out_block,
        vector, vector, vector, in_block, vector, out_block, vector, rows,
    )
    results = P("section", None, None, "gx", "gy")
    out_specs = (
        results, results, vector, vector, in_block, vector, in_block, in_block, vector,
        out_block, vector, vector, vector, in_block, vector, out_block, vector,
    )
    return jax.shard_map(local, mesh=mesh, in_specs=in_specs, out_specs=out_specs, check_vma=False)
```

```python
import jax
import jax.numpy as jnp
from jax import lax
from jax.experimental import pallas as pl
from jax.experimental.pallas import tpu as pltpu
from jax.sharding import PartitionSpec as P

BF = jnp.bfloat16
F32 = jnp.float32
SEQ = 577
EPS = 1e-06
NEG = -1e30
ROWS = 160
TOK = 80
LANES = 128
WIDE = 1024
MESH = pl.DeviceIdType.MESH

K_X, K_O, K_M, K_D, K_G, K_N2, K_GM, K_N1 = range(8)
V_AG, V_AS, V_MG, V_MS, V_BQ, V_BV, V_BO, V_BD, V_BU = range(9)


def dot_nn(a, b):
    return lax.dot_general(a, b, (((1,), (0,)), ((), ())), preferred_element_type=F32)


def dot_nt(a, b):
    return lax.dot_general(a, b, (((1,), (1,)), ((), ())), preferred_element_type=F32)


def dot_tn(a, b):
    return lax.dot_general(a, b, (((0,), (0,)), ((), ())), preferred_element_type=F32)


def lanes(index):
    return pl.ds(pl.multiple_of(index * LANES, LANES), LANES)


def wait_bytes(ref, sem):
    pltpu.make_async_copy(ref, ref, sem).wait()


def put(src, dst, send_sem, recv_sem, device):
    pltpu.make_async_remote_copy(
        src_ref=src,
        dst_ref=dst,
        send_sem=send_sem,
        recv_sem=recv_sem,
        device_id=device,
        device_id_type=MESH,
    ).start()


def image_rows(c):
    return pl.ds(c * TOK, TOK)


def row_sum(values):
    return jnp.sum(values, axis=0, keepdims=True)


def three_parts(values):
    high = values.astype(BF).astype(F32)
    rest = values - high
    mid = rest.astype(BF).astype(F32)
    return high, mid, rest - mid


def kernel(
    images, counts, attn_gain, attn_shift, w_query, b_query, w_key, w_value, b_value, w_out,
    b_out, mlp_gain, mlp_shift, w_up, b_up, w_down, b_down, cotangent,
    act_o, ig_o, g_attn_gain, g_attn_shift, g_w_query, g_b_query, g_w_key, g_w_value, g_b_value,
    g_w_out, g_b_out, g_mlp_gain, g_mlp_shift, g_w_up, g_b_up, g_w_down, g_b_down,
    vec, cot, wqkv, wo, wup, wdn,
    xg, mg, gg, gmg, norm, unit, rstd, res, mid, gcur, gmid,
    stage, rsb, stat, kv, qg, dog, owna, attn_f, attn_b, aux, hid, pre,
    grad_pre, ybuf, igbuf, s_vec, r_vec, vgrad,
    lsem, gy_send, gy_recv, st_send, st_recv, kv_send, kv_recv, do_send, do_recv,
    vec_send, vec_recv, wa1_send, wa1_recv, wa2_send, wa2_recv, wb1_send, wb1_recv, wb2_send,
    wb2_recv, ga1_send, ga1_recv, ga2_send, ga2_recv, gb1_send, gb1_recv, gb2_send, gb2_recv,
    v_send, v_recv, a_send, a_recv, i_send, i_recv, *grad_refs,
):
    staged, ra1, pa, ra2, rb1, pb, rb2 = [grad_refs[4 * n : 4 * n + 4] for n in range(7)]
    weights_at = (wqkv, wo, wup, wdn)
    s = lax.axis_index("section")
    gx = lax.axis_index("gx")
    gy = lax.axis_index("gy")
    other = 1 - s
    mine = lanes(gy)
    x = gx // 2
    h = lax.rem(gx, 2)
    y_slot = h * 2 + s

    barrier = pltpu.get_barrier_semaphore()

    def greet(device):
        pl.semaphore_signal(barrier, inc=1, device_id=device, device_id_type=MESH)

    gy_peers = [(s, gx, lax.rem(gy + k, 8)) for k in (4, 5, 3, 6, 2, 7, 1)]
    far_gx = [(other, lax.rem(gx + k, 8), gy) for k in range(8)]
    far_gy = [(other, gx, lax.rem(gy + k, 8)) for k in range(8)]
    x_peers = [(s, lax.rem(x + k, 4) * 2 + h, gy) for k in (2, 1, 3)]
    gx_peers = [
        (s, lax.rem(x + k, 4) * 2 + side, gy)
        for k, side in ((2, 1 - h), (1, 1 - h), (3, 1 - h), (2, h), (0, 1 - h), (1, h), (3, h))
    ]
    y_peers = [(s, x * 2 + 1 - h, gy), (other, gx, gy), (other, x * 2 + 1 - h, gy)]
    for device in gy_peers + gx_peers + far_gx + far_gy[1:]:
        greet(device)

    own = [pltpu.make_async_copy(images.at[s], xg.at[0, :, mine], lsem.at[0])]
    own.append(pltpu.make_async_copy(cotangent.at[s], cot, lsem.at[1]))
    rows = [attn_gain, attn_shift, mlp_gain, mlp_shift, b_query, b_value, b_out, b_down]
    vec_own = []
    for row, ref in enumerate(rows):
        vec_own.append(pltpu.make_async_copy(ref, vec.at[s, row, :, mine], lsem.at[8 + row]))
    for part in range(4):
        vec_own.append(
            pltpu.make_async_copy(
                b_up.at[:, part * LANES : (part + 1) * LANES],
                vec.at[s, V_BU + part, :, mine],
                lsem.at[16 + part],
            )
        )
    w_own = []
    for part, ref in enumerate((w_query, w_key, w_value)):
        w_own.append(
            pltpu.make_async_copy(
                ref, wqkv.at[s, x, h, :, part * LANES : (part + 1) * LANES], lsem.at[2 + part]
            )
        )
    w_own.append(pltpu.make_async_copy(w_out, wo.at[s, x, h], lsem.at[5]))
    w_own.append(pltpu.make_async_copy(w_up, wup.at[s, x, h], lsem.at[6]))
    w_own.append(pltpu.make_async_copy(w_down, wdn.at[s, x, h], lsem.at[7]))
    for copy in own + vec_own + w_own:
        copy.start()

    pl.semaphore_wait(barrier, 29)

    for c in range(2):
        for device in gy_peers:
            put(
                images.at[s, image_rows(c)],
                xg.at[0, image_rows(c), mine],
                gy_send.at[K_X, 0, c],
                gy_recv.at[K_X, 0, c],
                device,
            )
    for copy in vec_own:
        copy.wait()
    for near, group in ((0, gy_peers), (1, far_gy)):
        for device in group:
            block = vec.at[s, :, :, mine]
            put(block, block, vec_send.at[near], vec_recv.at[near], device)
    for copy in w_own:
        copy.wait()
    own[0].wait()
    own[1].wait()

    half_rows = (64, 64, 64, 256)

    def halves(group):
        return pl.ds(0, half_rows[group]), pl.ds(half_rows[group], half_rows[group])

    def spread_own(groups):
        for group in groups:
            ref = weights_at[group]
            first, second = halves(group)
            block = ref.at[s, x, h, first]
            for device in x_peers:
                put(block, block, wa1_send.at[group], wa1_recv.at[group], device)
            block = ref.at[s, x, h, second]
            for device in y_peers:
                put(block, block, wb1_send.at[group], wb1_recv.at[group, s], device)

    def pass_on(groups, l):
        for group in groups:
            ref = weights_at[group]
            first, second = halves(group)

            @pl.when(l == s)
            def _(ref=ref, first=first, group=group):
                wait_bytes(ref.at[l, 0:3, 0, first], wa1_recv.at[group])
                block = ref.at[s, :, h, first]
                for device in y_peers:
                    put(block, block, wa2_send.at[group], wa2_recv.at[group, s], device)
                wait_bytes(ref.at[l, 0, 0, first], wb1_recv.at[group, l])

            @pl.when(l != s)
            def _(ref=ref, first=first, group=group):
                wait_bytes(ref.at[l, 0, :, first], wb1_recv.at[group, l])

            block = ref.at[l, x, :, second]
            for device in x_peers:
                put(block, block, wb2_send.at[group, l], wb2_recv.at[group, l], device)

    def wait_weights(group, l):
        ref = weights_at[group]
        first, _ = halves(group)

        @pl.when(l == s)
        def _():
            wait_bytes(ref.at[l, :, 0, first], wa2_recv.at[group, l])

        @pl.when(l != s)
        def _():
            wait_bytes(ref.at[l, :, :, first], wa2_recv.at[group, l])

        wait_bytes(ref.at[l, 0:3, :, first], wb2_recv.at[group, l])

    def by_columns(ref, l):
        return jnp.concatenate([ref[l, a, b] for a in range(4) for b in range(2)], axis=1)

    @pl.when(s == 0)
    def _():
        spread_own((0, 1))

    def gather_gy(buffer, kind, l, c):
        block = buffer.at[l, image_rows(c), mine]
        for device in gy_peers:
            put(block, block, gy_send.at[kind, l, c], gy_recv.at[kind, l, c], device)

    def wait_gather(buffer, kind, l, c):
        wait_bytes(buffer.at[l, image_rows(c), 0:896], gy_recv.at[kind, l, c])

    slot_of = {K_O: 0, K_D: 1, K_N2: 2, K_N1: 3}

    def scatter_gy(partial, kind, l, c):
        slot = slot_of[kind]
        stage[slot, l, image_rows(c)] = partial.astype(BF)
        for _, _, peer in gy_peers:
            put(
                stage.at[slot, l, image_rows(c), lanes(peer)],
                rsb.at[slot, l, c, gy],
                gy_send.at[kind, l, c],
                gy_recv.at[kind, l, c],
                (s, gx, peer),
            )
        rsb[slot, l, c, gy] = stage[slot, l, image_rows(c), mine]

    def wait_scatter(kind, l, c):
        slot = slot_of[kind]
        wait_bytes(rsb.at[slot, l, c, 0:7], gy_recv.at[kind, l, c])
        total = rsb[slot, l, c, 0].astype(F32)
        for source in range(1, 8):
            total = total + rsb[slot, l, c, source].astype(F32)
        return total

    lane_id = lax.broadcasted_iota(jnp.int32, (TOK, LANES), 1)
    low_half = lane_id < 64
    head_mask = [low_half.astype(F32).astype(BF), (lane_id >= 64).astype(F32).astype(BF)]

    def two_heads(block):
        return jnp.concatenate([block * head_mask[0], block * head_mask[1]], axis=0)

    def join_heads(both):
        return jnp.where(low_half, both[:TOK], both[TOK:])

    def masked_lanes(low, count, value, height):
        ids = lax.broadcasted_iota(jnp.int32, (height, LANES), 1)
        return jnp.where((ids >= low) & (ids < low + count), value, 0.0).astype(BF)

    key_ok = lax.broadcasted_iota(jnp.int32, (ROWS, 640), 1) < SEQ

    def norm_rows(values, gain_row, shift_row, which, l, c):
        center = values - jnp.mean(values, axis=-1, keepdims=True)
        spread = jnp.mean(center * center, axis=-1, keepdims=True)
        scale = lax.rsqrt(spread + EPS)
        xhat = center * scale
        unit[which, l, image_rows(c)] = xhat
        rstd[which, l, image_rows(c)] = jnp.broadcast_to(scale, (TOK, LANES))
        normed = (xhat * vec[l, gain_row] + vec[l, shift_row]).astype(BF)
        norm[which, l, image_rows(c)] = normed
        return normed

    row_id = lax.broadcasted_iota(jnp.int32, (ROWS, LANES), 0)
    image_id = (row_id >= TOK).astype(jnp.int32)
    position = row_id - image_id * TOK + gx * TOK
    live = ((image_id < counts[s]) & (position < SEQ)).astype(F32)
    gcur[...] = cot[...].astype(F32) * live

    def start_gradient(l, c):
        grad_out = gcur[image_rows(c)]
        gg[l, image_rows(c), mine] = grad_out.astype(BF)
        gather_gy(gg, K_G, l, c)

    res[...] = xg[0, :, mine].astype(F32)
    wait_bytes(vec.at[s, :, :, 0:896], vec_recv.at[0])
    wait_bytes(vec.at[other], vec_recv.at[1])

    def finish_layer(l):
        for c in range(2):
            output = mid[image_rows(c)] + wait_scatter(K_D, l, c) + vec[l, V_BD, :, mine]
            output = output.astype(BF)
            ybuf[l, image_rows(c)] = output
            if l == 0:
                res[image_rows(c)] = output.astype(F32)
                xg[1, image_rows(c), mine] = output
                gather_gy(xg, K_X, 1, c)

        @pl.when(s == l)
        def _():
            pltpu.make_async_copy(ybuf.at[l], act_o.at[s], a_recv.at[0]).start()

        @pl.when(s != l)
        def _():
            put(ybuf.at[l], act_o.at[s], a_send.at[0], a_recv.at[0], (other, gx, gy))

    def forward(l, carry):
        for c in range(2):
            wait_gather(xg, K_X, l, c)
            normed = norm_rows(xg[l, image_rows(c)].astype(F32), V_AG, V_AS, 0, l, c)
            if c == 0:

                @pl.when(l == 0)
                def _():
                    pass_on((0,), 0)

                    @pl.when(s == 0)
                    def _():
                        spread_own((2, 3))

                    @pl.when(s == 1)
                    def _():
                        spread_own((0, 1, 2, 3))


                wait_weights(0, l)
            qkv = dot_nn(normed, wqkv[l].reshape(WIDE, 384))
            kv[l, 0, c, gx] = qkv[:, LANES : 2 * LANES].astype(BF)
            kv[l, 1, c, gx] = (qkv[:, 2 * LANES :] + vec[l, V_BV, :, mine]).astype(BF)
            query = (qkv[:, :LANES] + vec[l, V_BQ, :, mine]).astype(BF)
            qg[l, c, gx] = query * jnp.asarray(0.125, BF)
            for device in gx_peers:
                block = kv.at[l, :, c, gx]
                put(block, block, kv_send.at[0, l, c], kv_recv.at[0, l, c], device)
        @pl.when(l == 0)
        def _():
            pass_on((1, 2, 3), 0)
            pass_on((0, 1, 2, 3), 1)

        for device in gx_peers:
            block = qg.at[l, :, gx]
            put(block, block, kv_send.at[1, l, 0], kv_recv.at[1, l, 0], device)

        @pl.when(l == 1)
        def _():
            for c in range(2):
                start_gradient(1, c)

        later = []
        for c in range(2):
            wait_bytes(kv.at[l, :, c, 0:7], kv_recv.at[0, l, c])
            all_keys = kv[l, 0, c].reshape(640, LANES)
            all_values = kv[l, 1, c].reshape(640, LANES)
            scores = dot_nt(two_heads(qg[l, c, gx]), all_keys)
            scores = jnp.where(key_ok, scores, NEG)
            highest = jnp.max(scores, axis=-1, keepdims=True)
            exponent = jnp.exp(scores - highest)
            summed = jnp.sum(exponent, axis=-1, keepdims=True)
            full = exponent / summed
            weights = full.astype(BF)
            mixed = join_heads(dot_nn(weights, all_values))
            mixed_low = mixed.astype(BF)
            attn_b[l, image_rows(c)] = mixed_low
            if c == 0:
                wait_weights(1, l)
            scatter_gy(dot_nn(mixed_low, by_columns(wo, l)), K_O, l, c)
            later.append((c, full, weights, mixed, all_values, highest, summed))

        for c, full, weights, mixed, all_values, highest, summed in later:
            left_out = (full - weights.astype(F32)).astype(BF)
            attn_f[l, image_rows(c)] = mixed + join_heads(dot_nn(left_out, all_values))
            logs = highest + jnp.log(summed)
            line = jnp.zeros((TOK, LANES), F32)
            for head in range(2):
                for at, piece in enumerate(three_parts(logs[head * TOK : (head + 1) * TOK])):
                    line = jnp.where(lane_id == head * 3 + at, piece, line)
            aux[l, image_rows(c)] = line

        for c in range(2):
            middle = res[image_rows(c)] + wait_scatter(K_O, l, c) + vec[l, V_BO, :, mine]
            mid[image_rows(c)] = middle
            mg[l, image_rows(c), mine] = middle.astype(BF)
            gather_gy(mg, K_M, l, c)

        slopes = []
        bias = jnp.concatenate([vec[l, V_BU + n, :, mine] for n in range(4)], axis=1)
        for c in range(2):
            wait_gather(mg, K_M, l, c)
            normed = norm_rows(mg[l, image_rows(c)].astype(F32), V_MG, V_MS, 1, l, c)
            if c == 0:
                wait_weights(2, l)
            pre_act = dot_nn(normed, wup[l].reshape(WIDE, 512)) + bias
            gate = 0.5 * (1.0 + lax.erf(pre_act * 0.7071067811865476))
            hidden = (pre_act * gate).astype(BF)
            hid[l, image_rows(c)] = hidden
            if c == 0:
                wait_weights(3, l)
            scatter_gy(dot_nn(hidden, by_columns(wdn, l)), K_D, l, c)
            slopes.append((pre_act, gate))

        for c, (pre_act, gate) in enumerate(slopes):
            slope = jnp.exp(-0.5 * pre_act * pre_act) * 0.3989422804014327
            pre[l, image_rows(c)] = gate + pre_act * slope

        @pl.when(l == 0)
        def _():
            finish_layer(0)

        return carry

    lax.fori_loop(0, 2, forward, 0)

    def reduce_start(groups, l):
        for group in groups:
            first, second = halves(group)
            ref = staged[group]
            for _, peer, _ in x_peers:
                put(
                    ref.at[l, peer // 2, :, first],
                    ra1[group].at[l, x],
                    ga1_send.at[group, l],
                    ga1_recv.at[group, l],
                    (s, peer, gy),
                )
            put(
                ref.at[l, :, 1 - h, second],
                rb1[group].at[y_slot],
                gb1_send.at[group, l],
                gb1_recv.at[group],
                (l, x * 2 + 1 - h, gy),
            )

            @pl.when(l != s)
            def _(ref=ref, second=second, group=group):
                put(
                    ref.at[l, :, h, second],
                    rb1[group].at[y_slot],
                    gb1_send.at[group, l],
                    gb1_recv.at[group],
                    (l, gx, gy),
                )

            ra1[group][l, x] = ref[l, x, :, first]

            @pl.when(l == s)
            def _(ref=ref, second=second, group=group):
                rb1[group][y_slot] = ref[l, :, h, second]

    def four(ref, index=None):
        parts = [(ref[n] if index is None else ref[index, n]).astype(F32) for n in range(4)]
        return (parts[0] + parts[1]) + (parts[2] + parts[3])

    def reduce_turn(groups, l):
        for group in groups:
            wait_bytes(ra1[group].at[l, 0:3], ga1_recv.at[group, l])
            pa[group][l] = four(ra1[group], l).astype(BF)
            put(
                pa[group].at[l, 1 - h],
                ra2[group].at[y_slot],
                ga2_send.at[group, l],
                ga2_recv.at[group],
                (l, x * 2 + 1 - h, gy),
            )

            @pl.when(l != s)
            def _(group=group):
                put(
                    pa[group].at[l, h],
                    ra2[group].at[y_slot],
                    ga2_send.at[group, l],
                    ga2_recv.at[group],
                    (l, gx, gy),
                )

            @pl.when(l == s)
            def _(group=group):
                ra2[group][y_slot] = pa[group][l, h]
                wait_bytes(rb1[group].at[0:3], gb1_recv.at[group])
                pb[group][...] = four(rb1[group]).astype(BF)
                for _, peer, _ in x_peers:
                    put(
                        pb[group].at[peer // 2],
                        rb2[group].at[x],
                        gb2_send.at[group],
                        gb2_recv.at[group],
                        (s, peer, gy),
                    )
                rb2[group][x] = pb[group][x]

    def send_vec(l):
        for j in range(8):
            k = lax.rem(gx + j, 8)
            dst = r_vec.at[s * 8 + gx]
            if j == 0:

                @pl.when(l == s)
                def _():
                    r_vec[s * 8 + gx] = s_vec[l]

                @pl.when(l != s)
                def _(k=k):
                    put(s_vec.at[l], r_vec.at[s * 8 + gx], v_send.at[l], v_recv.at[0], (l, k, gy))

            else:
                put(s_vec.at[l], dst, v_send.at[l], v_recv.at[0], (l, k, gy))

    def send_stats(first, second, which, l, c):
        ids = lax.broadcasted_iota(jnp.int32, (TOK, LANES), 1)
        both = jnp.where(ids == 0, first, jnp.where(ids == 1, second, 0.0))
        both = jnp.concatenate([both, jnp.zeros((LANES - TOK, LANES), F32)], axis=0)
        stat[which, l, c, gy] = both.T[:8]
        for device in gy_peers:
            block = stat.at[which, l, c, gy]
            put(block, block, st_send.at[which, l, c], st_recv.at[which, l, c], device)

    def wait_stats(which, l, c):
        wait_bytes(stat.at[which, l, c, 0:7], st_recv.at[which, l, c])
        total = stat[which, l, c, 0]
        for source in range(1, 8):
            total = total + stat[which, l, c, source]
        total = jnp.concatenate([total, jnp.zeros((LANES - 8, LANES), F32)], axis=0).T
        return total[:TOK, 0:1], total[:TOK, 1:2]

    def norm_back_send(partial, which, gain_row, kind, l, c):
        scatter_gy(partial, kind, l, c)
        weighted = partial * vec[l, gain_row]
        first = jnp.sum(weighted, axis=-1, keepdims=True)
        second = jnp.sum(weighted * unit[which, l, image_rows(c)], axis=-1, keepdims=True)
        send_stats(first, second, which, l, c)

    def add_vec(slot, value, c):
        if c == 0:
            vgrad[slot] = value
        else:
            vgrad[slot] += value

    def norm_back_take(which, gain_row, kind, l, c, gain_slot, shift_slot):
        grad = wait_scatter(kind, l, c)
        first, second = wait_stats(which, l, c)
        xhat = unit[which, l, image_rows(c), mine]
        add_vec(gain_slot, row_sum(grad * xhat), c)
        add_vec(shift_slot, row_sum(grad), c)
        inner = grad * vec[l, gain_row, :, mine]
        return rstd[which, l, image_rows(c)] * (
            inner - first * (1.0 / WIDE) - xhat * (second * (1.0 / WIDE))
        )

    def store_columns(group, grad, l):
        for block in range(8):
            columns = grad[:, block * LANES : (block + 1) * LANES]
            staged[group][l, block // 2, block % 2] = columns.astype(BF)

    key_side = masked_lanes(0, 6, -1.0, 640)
    value_side = masked_lanes(6, 6, -1.0, 640)
    row_ids = lax.broadcasted_iota(jnp.int32, (ROWS, 640), 0)
    key_pos = jnp.where(row_ids >= TOK, row_ids - TOK, row_ids) + gx * TOK
    own_ok = key_pos < SEQ
    def backward(step, carry):
        l = 1 - step
        vgrad[V_BD] = row_sum(gcur[...])
        for c in range(2):
            wait_gather(gg, K_G, l, c)
            grad_hid = dot_nt(gg[l, image_rows(c)], by_columns(wdn, l))
            low = (grad_hid * pre[l, image_rows(c)]).astype(BF)
            grad_pre[image_rows(c)] = low
            norm_back_send(
                dot_nt(low, wup[l].reshape(WIDE, 512)), 1, V_MG, K_N2, l, c
            )
        up_sum = row_sum(grad_pre[...].astype(F32))
        for n in range(4):
            vgrad[V_BU + n] = up_sum[:, n * LANES : (n + 1) * LANES]
        store_columns(3, dot_tn(hid[l], gg[l]), l)
        reduce_start((3,), l)

        @pl.when(l == 0)
        def _():
            reduce_turn((0,), 1)

        @pl.when(l == 1)
        def _():
            finish_layer(1)

        for c in range(2):
            grad_mid = gcur[image_rows(c)] + norm_back_take(1, V_MG, K_N2, l, c, V_MG, V_MS)
            gmid[image_rows(c)] = grad_mid
            gmg[l, image_rows(c), mine] = grad_mid.astype(BF)
            gather_gy(gmg, K_GM, l, c)
        staged[2][l] = dot_tn(norm[1, l], grad_pre[...]).astype(BF).reshape(4, 2, LANES, 512)
        reduce_start((2,), l)
        vgrad[V_BO] = row_sum(gmid[...])
        for c in range(2):
            wait_gather(gmg, K_GM, l, c)
            grad_mixed = dot_nt(gmg[l, image_rows(c)], by_columns(wo, l)).astype(BF)
            product = grad_mixed.astype(F32) * attn_f[l, image_rows(c)]
            line = aux[l, image_rows(c)]
            for head in range(2):
                picked = jnp.where(low_half == (head == 0), product, 0.0)
                delta = jnp.sum(picked, axis=-1, keepdims=True)
                for at, piece in enumerate(three_parts(delta)):
                    line = jnp.where(lane_id == 6 + head * 3 + at, piece, line)
            dog[l, c, gx, :, 0:LANES] = grad_mixed
            dog[l, c, gx, :, LANES:] = line.astype(BF)
            for device in gx_peers:
                block = dog.at[l, c, gx]
                put(block, block, do_send.at[l, c], do_recv.at[l, c], device)
        store_columns(1, dot_tn(attn_b[l], gmg[l]), l)
        reduce_start((1,), l)
        reduce_turn((3,), l)

        @pl.when(l == 1)
        def _():
            wait_bytes(qg.at[0, :, 0:7], kv_recv.at[1, 0, 0])
            wait_bytes(qg.at[1, :, 0:7], kv_recv.at[1, 1, 0])

        for c in range(2):
            wait_bytes(dog.at[l, c, 0:7], do_recv.at[l, c])
            all_keys = kv[l, 0, c].reshape(640, LANES)
            all_values = kv[l, 1, c].reshape(640, LANES)
            all_query = qg[l, c].reshape(640, LANES)
            all_grads = dog[l, c].reshape(640, 2 * LANES)
            all_aux = all_grads[:, LANES:]
            all_mixed = all_grads[:, :LANES]
            my_aux = dog[l, c, gx, :, LANES:]
            my_log = jnp.concatenate(
                [my_aux * masked_lanes(0, 3, 1.0, TOK), my_aux * masked_lanes(3, 3, 1.0, TOK)],
                axis=0,
            )
            my_delta = jnp.concatenate(
                [my_aux * masked_lanes(6, 3, 1.0, TOK), my_aux * masked_lanes(9, 3, 1.0, TOK)],
                axis=0,
            )
            my_query = jnp.concatenate([two_heads(qg[l, c, gx]), my_log], axis=1)
            my_mixed = jnp.concatenate([two_heads(dog[l, c, gx, :, 0:LANES]), my_delta], axis=1)
            scores = dot_nt(my_query, jnp.concatenate([all_keys, key_side], axis=1))
            weights = jnp.exp(jnp.where(key_ok, scores, NEG))
            inner = dot_nt(my_mixed, jnp.concatenate([all_values, value_side], axis=1))
            grad_scores = (weights * inner).astype(BF)
            grad_query = join_heads(dot_nn(grad_scores, all_keys)) * 0.125
            owna[image_rows(c), 0:LANES] = grad_query.astype(BF)

            key_log = jnp.concatenate(
                [masked_lanes(0, 3, -1.0, TOK), masked_lanes(3, 3, -1.0, TOK)], axis=0
            )
            key_delta = jnp.concatenate(
                [masked_lanes(6, 3, -1.0, TOK), masked_lanes(9, 3, -1.0, TOK)], axis=0
            )
            my_key = jnp.concatenate([two_heads(kv[l, 0, c, gx]), key_log], axis=1)
            my_value = jnp.concatenate([two_heads(kv[l, 1, c, gx]), key_delta], axis=1)
            scores = dot_nt(my_key, jnp.concatenate([all_query, all_aux], axis=1))
            weights = jnp.exp(jnp.where(own_ok, scores, NEG))
            inner = dot_nt(my_value, all_grads)
            grad_scores = (weights * inner).astype(BF)
            grad_key = join_heads(dot_nn(grad_scores, all_query))
            grad_value = join_heads(dot_nn(weights.astype(BF), all_mixed))
            owna[image_rows(c), LANES : 2 * LANES] = grad_key.astype(BF)
            owna[image_rows(c), 2 * LANES :] = grad_value.astype(BF)
            norm_back_send(
                dot_nt(owna[image_rows(c)], wqkv[l].reshape(WIDE, 384)), 0, V_AG, K_N1, l, c
            )
        staged[0][l] = dot_tn(norm[0, l], owna[...]).astype(BF).reshape(4, 2, LANES, 384)
        reduce_start((0,), l)
        reduce_turn((2, 1), l)
        bias_sum = row_sum(owna[...].astype(F32))
        vgrad[V_BQ] = bias_sum[:, :LANES]
        vgrad[V_BV] = bias_sum[:, 2 * LANES :]
        for c in range(2):
            grad_in = gmid[image_rows(c)] + norm_back_take(0, V_AG, K_N1, l, c, V_AG, V_AS)
            igbuf[l, image_rows(c)] = grad_in
            gcur[image_rows(c)] = grad_in.astype(BF).astype(F32)

            @pl.when(l == 1)
            def _(c=c):
                start_gradient(0, c)

        s_vec[l] = vgrad[...]
        send_vec(l)

        @pl.when(l == s)
        def _():
            pltpu.make_async_copy(igbuf.at[l], ig_o.at[s], i_recv.at[0]).start()

        @pl.when(l != s)
        def _():
            put(igbuf.at[l], ig_o.at[s], i_send.at[0], i_recv.at[0], (other, gx, gy))

        @pl.when(l == 0)
        def _():
            reduce_turn((0,), 0)

        return carry

    lax.fori_loop(0, 2, backward, 0)

    def sum_of(ref):
        total = ref[0].astype(F32)
        for source in range(1, 16):
            total = total + ref[source].astype(F32)
        return total

    def final_sum(group):
        first, second = halves(group)
        wait_bytes(ra2[group].at[0:3], ga2_recv.at[group])
        wait_bytes(rb2[group].at[0:3], gb2_recv.at[group])
        return jnp.concatenate([four(ra2[group]), four(rb2[group])], axis=0)

    g_w_down[...] = final_sum(3)
    g_w_up[...] = final_sum(2)
    g_w_out[...] = final_sum(1)
    wait_bytes(ybuf.at[0], a_send.at[0])
    wait_bytes(igbuf.at[0], i_send.at[0])
    wait_bytes(vec.at[s, :, :, 0:896], vec_send.at[0])
    wait_bytes(vec.at[s], vec_send.at[1])
    for group in range(4):
        ref = weights_at[group]
        first, _ = halves(group)
        wait_bytes(ref.at[0, 0:3, 0, first], wa1_send.at[group])
        wait_bytes(ref.at[0, 0:3, 0, first], wb1_send.at[group])
        wait_bytes(ref.at[0, 0:3], wa2_send.at[group])
        wait_bytes(rb2[group].at[0:3], gb2_send.at[group])
        for l in range(2):
            wait_bytes(ref.at[0, 0:3, :, first], wb2_send.at[group, l])
            wait_bytes(ra1[group].at[l, 0:3], ga1_send.at[group, l])
    for l in range(2):
        for c in range(2):
            for kind, buffer in ((K_X, xg), (K_M, mg), (K_G, gg), (K_GM, gmg)):
                wait_bytes(buffer.at[l, image_rows(c), 0:896], gy_send.at[kind, l, c])
            for kind, slot in slot_of.items():
                wait_bytes(rsb.at[slot, l, c, 0:7], gy_send.at[kind, l, c])
            for which in range(2):
                wait_bytes(stat.at[which, l, c, 0:7], st_send.at[which, l, c])
            wait_bytes(kv.at[l, :, c, 0:7], kv_send.at[0, l, c])
            wait_bytes(dog.at[l, c, 0:7], do_send.at[l, c])
        wait_bytes(qg.at[l, :, 0:7], kv_send.at[1, l, 0])
        for count, at in ((1, l), (2, 1 - l)):

            @pl.when(s == at)
            def _(l=l, count=count):
                for group in range(4):
                    wait_bytes(ra2[group].at[0:count], ga2_send.at[group, l])
                    wait_bytes(rb1[group].at[0:count], gb1_send.at[group, l])
                wait_bytes(r_vec.at[0 : 6 + count], v_send.at[l])

    total = final_sum(0)
    g_w_query[...] = total[:, :LANES]
    g_w_key[...] = total[:, LANES : 2 * LANES]
    g_w_value[...] = total[:, 2 * LANES :]
    wait_bytes(r_vec.at[0:15], v_recv.at[0])
    total = sum_of(r_vec)
    g_attn_gain[...] = total[V_AG]
    g_attn_shift[...] = total[V_AS]
    g_mlp_gain[...] = total[V_MG]
    g_mlp_shift[...] = total[V_MS]
    g_b_query[...] = total[V_BQ]
    g_b_value[...] = total[V_BV]
    g_b_out[...] = total[V_BO]
    g_b_down[...] = total[V_BD]
    for part in range(4):
        g_b_up[:, part * LANES : (part + 1) * LANES] = total[V_BU + part]
    wait_bytes(act_o, a_recv.at[0])
    wait_bytes(ig_o, i_recv.at[0])


def write_out(*refs):
    copies = [
        pltpu.make_async_copy(refs[n], refs[17 + n], refs[34].at[n]) for n in range(17)
    ]
    for copy in copies:
        copy.start()
    for copy in copies:
        copy.wait()


def finish(values):
    return pl.pallas_call(
        write_out,
        out_shape=[jax.ShapeDtypeStruct(value.shape, value.dtype) for value in values],
        in_specs=[pl.BlockSpec(memory_space=pltpu.VMEM)] * 17,
        out_specs=[pl.BlockSpec(memory_space=pl.ANY)] * 17,
        scratch_shapes=[pltpu.SemaphoreType.DMA((17,))],
        name="write_results",
    )(*values)


def local(
    images, counts, attn_gain, attn_shift, w_query, b_query, w_key, w_value, b_value, w_out,
    b_out, mlp_gain, mlp_shift, w_up, b_up, w_down, b_down, cotangent,
):
    anywhere = pl.BlockSpec(memory_space=pl.ANY)
    in_vmem = pl.BlockSpec(memory_space=pltpu.VMEM)
    in_smem = pl.BlockSpec(memory_space=pltpu.SMEM)
    in_specs = [anywhere, in_smem] + [anywhere] * 16
    row = jax.ShapeDtypeStruct((1, LANES), F32)
    square = jax.ShapeDtypeStruct((LANES, LANES), F32)
    out_shape = [
        jax.ShapeDtypeStruct((2, ROWS, LANES), BF),
        jax.ShapeDtypeStruct((2, ROWS, LANES), F32),
        row, row, square, row, square, square, row, square, row, row, row,
        jax.ShapeDtypeStruct((LANES, 512), F32),
        jax.ShapeDtypeStruct((1, 512), F32),
        jax.ShapeDtypeStruct((512, LANES), F32),
        row,
    ]
    vmem = pltpu.VMEM
    scratch = [
        vmem((2, 12, 1, WIDE), F32),
        vmem((ROWS, LANES), BF),
        vmem((2, 4, 2, LANES, 384), BF),
        vmem((2, 4, 2, LANES, LANES), BF),
        vmem((2, 4, 2, LANES, 512), BF),
        vmem((2, 4, 2, 512, LANES), BF),
        vmem((2, ROWS, WIDE), BF),
        vmem((2, ROWS, WIDE), BF),
        vmem((2, ROWS, WIDE), BF),
        vmem((2, ROWS, WIDE), BF),
        vmem((2, 2, ROWS, WIDE), BF),
        vmem((2, 2, ROWS, WIDE), F32),
        vmem((2, 2, ROWS, LANES), F32),
        vmem((ROWS, LANES), F32),
        vmem((ROWS, LANES), F32),
        vmem((ROWS, LANES), F32),
        vmem((ROWS, LANES), F32),
        vmem((4, 2, ROWS, WIDE), BF),
        vmem((4, 2, 2, 8, TOK, LANES), BF),
        vmem((2, 2, 2, 8, 8, LANES), F32),
        vmem((2, 2, 2, 8, TOK, LANES), BF),
        vmem((2, 2, 8, TOK, LANES), BF),
        vmem((2, 2, 8, TOK, 2 * LANES), BF),
        vmem((ROWS, 384), BF),
        vmem((2, ROWS, LANES), F32),
        vmem((2, ROWS, LANES), BF),
        vmem((2, ROWS, LANES), F32),
        vmem((2, ROWS, 512), BF),
        vmem((2, ROWS, 512), F32),
        vmem((ROWS, 512), BF),
        vmem((2, ROWS, LANES), BF),
        vmem((2, ROWS, LANES), F32),
        vmem((2, 12, 1, LANES), F32),
        vmem((16, 12, 1, LANES), F32),
        vmem((12, 1, LANES), F32),
        pltpu.SemaphoreType.DMA((20,)),
        pltpu.SemaphoreType.DMA((8, 2, 2)),
        pltpu.SemaphoreType.DMA((8, 2, 2)),
        pltpu.SemaphoreType.DMA((2, 2, 2)),
        pltpu.SemaphoreType.DMA((2, 2, 2)),
        pltpu.SemaphoreType.DMA((2, 2, 2)),
        pltpu.SemaphoreType.DMA((2, 2, 2)),
        pltpu.SemaphoreType.DMA((2, 2)),
        pltpu.SemaphoreType.DMA((2, 2)),
        pltpu.SemaphoreType.DMA((2,)),
        pltpu.SemaphoreType.DMA((2,)),
        pltpu.SemaphoreType.DMA((4,)),
        pltpu.SemaphoreType.DMA((4,)),
        pltpu.SemaphoreType.DMA((4,)),
        pltpu.SemaphoreType.DMA((4, 2)),
        pltpu.SemaphoreType.DMA((4,)),
        pltpu.SemaphoreType.DMA((4, 2)),
        pltpu.SemaphoreType.DMA((4, 2)),
        pltpu.SemaphoreType.DMA((4, 2)),
        pltpu.SemaphoreType.DMA((4, 2)),
        pltpu.SemaphoreType.DMA((4, 2)),
        pltpu.SemaphoreType.DMA((4, 2)),
        pltpu.SemaphoreType.DMA((4,)),
        pltpu.SemaphoreType.DMA((4, 2)),
        pltpu.SemaphoreType.DMA((4,)),
        pltpu.SemaphoreType.DMA((4,)),
        pltpu.SemaphoreType.DMA((4,)),
        pltpu.SemaphoreType.DMA((2,)),
        pltpu.SemaphoreType.DMA((1,)),
        pltpu.SemaphoreType.DMA((1,)),
        pltpu.SemaphoreType.DMA((1,)),
        pltpu.SemaphoreType.DMA((1,)),
        pltpu.SemaphoreType.DMA((1,)),
    ]
    halved = [(64, 384), (64, LANES), (64, 512), (256, LANES)]
    for lead in (None, (2, 4, 2), (2, 2), (4,), (4, 4), (4,), (4,)):
        for rows, columns in halved:
            if lead is None:
                scratch.append(vmem((2, 4, 2, 2 * rows, columns), BF))
            else:
                scratch.append(vmem(lead + (rows, columns), BF))
    outs = pl.pallas_call(
        kernel,
        out_shape=out_shape,
        in_specs=in_specs,
        out_specs=[in_vmem] * 17,
        scratch_shapes=scratch,
        compiler_params=pltpu.CompilerParams(
            collective_id=0, has_side_effects=True, vmem_limit_bytes=58 * 1024 * 1024
        ),
        cost_estimate=pl.CostEstimate(
            flops=4_000_000_000, bytes_accessed=8_000_000, transcendentals=4_000_000
        ),
        name="two_sections",
    )(
        images.reshape(2, ROWS, LANES), counts, attn_gain, attn_shift, w_query[0], b_query,
        w_key[0], w_value[0], b_value, w_out[0], b_out, mlp_gain, mlp_shift, w_up[0], b_up,
        w_down[0], b_down, cotangent.reshape(2, ROWS, LANES),
    )
    outs = list(finish(outs))
    shape = (1,) + images.shape
    outs[0] = outs[0].reshape(shape)
    outs[1] = outs[1].reshape(shape)
    for index in (4, 6, 7, 9, 13, 15):
        outs[index] = outs[index][None]
    return tuple(outs)


def solution(mesh):
    vector = P("section", "gy")
    in_block = P("section", "gx", "gy")
    out_block = P("section", "gy", "gx")
    rows = P(None, None, "gx", "gy")
    in_specs = (
        rows, P(), vector, vector, in_block, vector, in_block, in_block, vector, out_block,
        vector, vector, vector, in_block, vector, out_block, vector, rows,
    )
    results = P("section", None, None, "gx", "gy")
    out_specs = (
        results, results, vector, vector, in_block, vector, in_block, in_block, vector,
        out_block, vector, vector, vector, in_block, vector, out_block, vector,
    )
    return jax.shard_map(local, mesh=mesh, in_specs=in_specs, out_specs=out_specs, check_vma=False)
```
